32 devices in a mesh: state: 4 (over x, core), row: 8 (over z, y).
Axes of the slice: x: 2, y: 2, z: 4, core: 2. Of those that a mesh axis runs over, the one named last changes fastest.
Arguments:
- vectors: bfloat16 [32768, 512], P('row', 'state'), as said below
- active: int32 [8], replicated, may hold values 0 or 1
Outputs:
- orthonormal: bfloat16 [32768, 512], P('row', 'state')
The draws below stay inside these ranges and needn't reach their ends.
Inputs may be any that keep to these rules, and one draw needn't show every extreme that they name: Each row and each column of vectors has its own scale.
All inputs are finite; a program needn't handle non-finite values.
Results may differ from the reference program's by a relative error of at most 0.00096.
Values may be sent and summed in bfloat16 or wider, within the bound.
No kernel may reach another device: no remote copies, remote signals or barrier semaphores. Data moves between devices by JAX's collectives and lax.ppermute only.
A program may use at most 64 MiB of HBM per device.

```python
import jax
import jax.numpy as jnp
from jax import lax

STATES = 8
VECS = 64
ITERS = 5
COLS = 512
ROWS = 32768


def draw_vectors(key, part):
    keys = jax.random.split(jax.random.fold_in(key, 11), 4)
    base = jax.random.normal(keys[0], (ROWS, COLS), jnp.float32)
    shuffle = jax.random.permutation(keys[1], COLS)
    mixed = base + 0.5 * base[:, shuffle]
    position = jnp.arange(ROWS).astype(jnp.float32) / ROWS
    ramp = jnp.exp(jnp.log(32.0) * (position - 0.5))
    col_scale = jnp.exp(jax.random.uniform(keys[2], (COLS,), jnp.float32, jnp.log(0.5), jnp.log(2.0)))
    row_scale = jnp.exp(jax.random.uniform(keys[3], (ROWS,), jnp.float32, 0.0, jnp.log(4.0)))
    return (mixed * col_scale[None, :] * (row_scale * ramp)[:, None]).astype(jnp.bfloat16)


def with_ends(values, stream_key, smallest, high):
    place = [jax.random.randint(jax.random.fold_in(stream_key, axis), (), 0, length) for axis, length in enumerate(values.shape)]
    main_axis = values.shape.index(max(values.shape))
    next_to = place[:main_axis] + [(place[main_axis] + 1) % values.shape[main_axis]] + place[main_axis + 1:]
    return values.at[tuple(place)].set(smallest).at[tuple(next_to)].set(high)


def setup_inputs(seed: int = 0) -> dict:
    key_of = jax.random.split(jax.random.key(seed), 3)
    return {
        "vectors": draw_vectors(jax.random.fold_in(key_of[2], 71), 0),
        "active": with_ends((jax.random.randint(key_of[1], (STATES,), 0, 4) < 3).astype(jnp.int32), jax.random.fold_in(key_of[1], 1), 0, 1),
    }


def newton_schulz(gram_matrix):
    identity = jnp.eye(gram_matrix.shape[0], dtype=jnp.float32)
    frob_norm = jnp.sqrt(jnp.sum(gram_matrix * gram_matrix))
    current = gram_matrix / frob_norm
    inverse = identity
    for repeat in range(ITERS):
        newton_step = 0.5 * (3.0 * identity - jnp.dot(inverse, current, precision=lax.Precision.HIGHEST))
        current = jnp.dot(current, newton_step, precision=lax.Precision.HIGHEST)
        inverse = jnp.dot(newton_step, inverse, precision=lax.Precision.HIGHEST)
    return (inverse * jnp.sqrt(ROWS / frob_norm)).astype(jnp.bfloat16)

def reference(vectors, active):
    flag_cols = jnp.repeat(active.astype(jnp.float32), VECS)
    masked = vectors * flag_cols.astype(jnp.bfloat16)
    gram_matrix = lax.dot_general(masked, masked, (((0,), (0,)), ((), ())), preferred_element_type=jnp.float32)
    gram_matrix = gram_matrix + jnp.diag((1.0 - flag_cols) * ROWS)
    factor = newton_schulz(gram_matrix)
    result = jnp.dot(masked, factor, preferred_element_type=jnp.float32)
    result = result + (1.0 - flag_cols) * vectors.astype(jnp.float32)
    return result.astype(jnp.bfloat16)
```

```python
import functools

import jax
import jax.numpy as jnp
from jax import lax
from jax.experimental import pallas as pl
from jax.experimental.pallas import tpu as pltpu
from jax.sharding import PartitionSpec as P

ITERS = 5
VMEM_BYTES = 40 * 1024 * 1024
F32 = jnp.float32
BF16 = jnp.bfloat16


def dot(left, right):
    return jnp.dot(left, right, preferred_element_type=F32)


def cross(left, right):
    return lax.dot_general(left, right, (((0,), (0,)), ((), ())), preferred_element_type=F32)


def call(kernel, out_shape, n_smem, n_args, flops, name, scratch=(), in_specs=None, out_specs=None):
    smem = pl.BlockSpec(memory_space=pltpu.SMEM)
    vmem = pl.BlockSpec(memory_space=pltpu.VMEM)
    return pl.pallas_call(
        kernel,
        out_shape=out_shape,
        in_specs=in_specs or [smem] * n_smem + [vmem] * n_args,
        out_specs=out_specs or jax.tree.map(lambda _: vmem, out_shape),
        scratch_shapes=list(scratch),
        compiler_params=pltpu.CompilerParams(vmem_limit_bytes=VMEM_BYTES),
        cost_estimate=pl.CostEstimate(flops=flops, bytes_accessed=4 * 2**20, transcendentals=0),
        name=name,
    )


def chip_gram_kernel(place, own, mate, slab):
    core = place[1]
    width = own.shape[1]
    slab[pl.ds(pl.multiple_of(core * width, width), width), :] = cross(own[...], own[...])
    slab[pl.ds(pl.multiple_of((1 - core) * width, width), width), :] = cross(own[...], mate[...])


def pair_gram_kernel(place, own, mate, across, slab, later):
    chip = place[0]
    half, width = across.shape
    rows = pl.ds(pl.multiple_of(chip * half, half), half)
    left = own[rows, :]
    later[...] = left
    same = cross(across[...], left)
    other = cross(across[...], mate[rows, :])
    slab[0:width, :] = jnp.where(chip == 0, same.T, same)
    slab[width : 2 * width, :] = jnp.where(chip == 0, other.T, other)


def sum_kernel(chip_parts, pair_parts, total):
    count = total.shape[0] // 2
    total[0:count, :] = jnp.sum(chip_parts[...], axis=0)
    total[count : 2 * count, :] = jnp.sum(pair_parts[...], axis=0)


def spread_kernel(place, mine, theirs, spread):
    chip = place[0]
    count = mine.shape[0] // 2
    chip_mine, chip_theirs = mine[0:count, :], theirs[0:count, :]
    first = jnp.where(chip == 0, chip_mine, chip_theirs)
    second = jnp.where(chip == 0, chip_theirs, chip_mine)
    pair = mine[count : 2 * count, :] + theirs[count : 2 * count, :]
    for row in range(spread.shape[0]):
        spread[row, 0] = first
        spread[row, 1] = second
        spread[row, 2] = pair


def split(value):
    high = value.astype(BF16)
    return high, (value - high.astype(F32)).astype(BF16)


def product(left, right):
    return dot(left[0], right[0]) + (dot(left[0], right[1]) + dot(left[1], right[0]))


def finish_kernel(
    total_rows, place, active, gram_mine, gram_mate, own, mate, across1, mate1, across2, mate2,
    out, gram, highs, lows, factor, left, sems,
):
    chip, core = place[0], place[1]
    half, width = across1.shape
    cols = gram.shape[0]
    near, far = pl.multiple_of(chip * half, half), pl.multiple_of((1 - chip) * half, half)
    copies = [
        pltpu.make_async_copy(own, left.at[:, 0:width], sems.at[0]),
        pltpu.make_async_copy(mate, left.at[:, width : 2 * width], sems.at[1]),
        pltpu.make_async_copy(across1, left.at[pl.ds(near, half), 2 * width : 3 * width], sems.at[2]),
        pltpu.make_async_copy(mate1, left.at[pl.ds(near, half), 3 * width : 4 * width], sems.at[3]),
        pltpu.make_async_copy(across2, left.at[pl.ds(far, half), 2 * width : 3 * width], sems.at[4]),
        pltpu.make_async_copy(mate2, left.at[pl.ds(far, half), 3 * width : 4 * width], sems.at[5]),
    ]
    for copy in copies:
        copy.start()

    def parts(index):
        mine = gram_mine[:, index].reshape(2 * width, width)
        theirs = gram_mate[:, index].reshape(2 * width, width)
        core0 = jnp.where(core == 0, mine, theirs)
        core1 = jnp.where(core == 0, theirs, mine)
        return core0[:width], core0[width:], core1[:width], core1[width:]

    def put(row, col, value):
        gram[row * width : (row + 1) * width, col * width : (col + 1) * width] = value

    for side in range(2):
        top0, low0, top1, low1 = parts(side)
        put(2 * side, 2 * side, top0)
        put(2 * side + 1, 2 * side, top1)
        put(2 * side, 2 * side + 1, jnp.where(chip == side, low0, low1))
        put(2 * side + 1, 2 * side + 1, jnp.where(chip == side, low1, low0))
    top0, low0, top1, low1 = parts(2)
    off10 = jnp.where(chip == 0, low0, low1)
    off01 = jnp.where(chip == 0, low1, low0)
    put(0, 2, top0)
    put(1, 3, top1)
    put(0, 3, off01)
    put(1, 2, off10)
    put(2, 0, top0.T)
    put(3, 1, top1.T)
    put(3, 0, off01.T)
    put(2, 1, off10.T)

    states = active.shape[0]
    vecs = cols // states
    col_state = lax.broadcasted_iota(jnp.int32, (1, cols), 1) // vecs
    flags = jnp.zeros((1, cols), F32)
    for state in range(states):
        flags = jnp.where(col_state == state, active[state].astype(F32), flags)
    square = jnp.zeros((vecs, cols), F32)
    for state in range(states):
        rows = slice(state * vecs, (state + 1) * vecs)
        kept = jnp.where(jnp.logical_and(flags != 0, active[state] != 0), gram[rows, :], 0.0)
        diagonal = lax.broadcasted_iota(jnp.int32, (vecs, cols), 0) + state * vecs == lax.broadcasted_iota(
            jnp.int32, (vecs, cols), 1
        )
        kept = kept + jnp.where(diagonal, (1.0 - flags) * total_rows, 0.0)
        gram[rows, :] = kept
        square = square + kept * kept
    frob_square = jnp.sum(jnp.sum(square, axis=0, keepdims=True), axis=1, keepdims=True)
    frob_norm = jnp.sqrt(frob_square)
    inverse_norm = 1.0 / frob_norm

    current = gram[...] * inverse_norm
    mine = pl.ds(pl.multiple_of((2 * chip + core) * width, width), width)
    for step in range(ITERS - 1):
        high, low = split(current)
        highs[step], lows[step] = high, low
        if step == ITERS - 2:
            gram[...] = current
            break
        square = product((high, low), (high, low))
        cube = product((high, low), split(square))
        current = 2.25 * current - 1.5 * square + 0.25 * cube

    def times(step, slab):
        return product((highs[step], lows[step]), split(slab))

    def newton(step, slab):
        return 1.5 * slab - 0.5 * times(step, slab)

    row_id = lax.broadcasted_iota(jnp.int32, (cols, width), 0)
    col_id = lax.broadcasted_iota(jnp.int32, (cols, width), 1) + (2 * chip + core) * width
    unit = jnp.where(row_id == col_id, 1.0, 0.0)
    last = ITERS - 2
    slab = 1.5 * unit - 0.5 * gram[:, mine]
    slab = 1.5 * unit - 0.5 * times(last, newton(last, slab))
    for step in range(last, -1, -1):
        slab = newton(step, slab)
    slab = slab * jnp.sqrt(total_rows / frob_norm)

    for state in range(states):
        rows = slice(state * vecs, (state + 1) * vecs)
        factor[rows, :] = jnp.where(active[state] != 0, slab[rows, :], unit[rows, :]).astype(BF16)

    def block(index):
        return factor[pl.ds(pl.multiple_of(index * width, width), width), :]

    weights = jnp.concatenate(
        [
            block(2 * chip + core),
            block(2 * chip + 1 - core),
            block(2 * (1 - chip) + core),
            block(2 * (1 - chip) + 1 - core),
        ],
        axis=0,
    )
    for copy in copies:
        copy.wait()
    out[...] = dot(left[...], weights).astype(BF16)


def shards(vectors, active):
    rows, width = vectors.shape
    half = rows // 2
    row_devices = lax.axis_size("row")
    total_rows = rows * row_devices
    cols = width * lax.axis_size("state")
    state = lax.axis_index("state")
    chip, core = state // 2, state % 2
    place = jnp.stack([chip, core]).astype(jnp.int32)
    count = 2 * width // row_devices
    shape = jax.ShapeDtypeStruct

    def swap(value, bit):
        return lax.ppermute(value, "state", [(index, index ^ bit) for index in range(4)])

    def exchange(value):
        return lax.all_to_all(value, "row", 0, 0, tiled=True)

    across1 = swap(lax.dynamic_slice_in_dim(vectors, (1 - chip) * half, half, 0), 2)
    mate = swap(vectors, 1)

    slab = shape((2 * width, width), F32)
    chip_slab = call(chip_gram_kernel, slab, 1, 2, 4 * rows * width * width, "chip_gram")(place, vectors, mate)
    chip_parts = exchange(chip_slab)

    pair_slab, later = call(
        pair_gram_kernel, (slab, shape((half, width), BF16)), 1, 3, 4 * half * width * width, "pair_gram"
    )(place, vectors, mate, across1)
    across2 = swap(later, 2)
    pair_parts = exchange(pair_slab)

    summed = call(sum_kernel, shape((2 * count, width), F32), 0, 2, 0, "sum_parts")(
        chip_parts.reshape(row_devices, count, width), pair_parts.reshape(row_devices, count, width)
    )
    route = [
        (place_from * row_devices + row, (place_from ^ (2 if row < row_devices // 2 else 3)) * row_devices + row)
        for place_from in range(4)
        for row in range(row_devices)
    ]
    theirs = lax.ppermute(summed, ("state", "row"), route)
    spread = call(spread_kernel, shape((row_devices, 3, count, width), F32), 1, 2, 0, "spread_parts")(
        place, summed, theirs
    )
    gram_mine = exchange(spread.reshape(row_devices * 3 * count, width))
    gram_mate = swap(gram_mine, 1)
    mate1 = swap(across1, 1)
    mate2 = swap(across2, 1)

    smem = pl.BlockSpec(memory_space=pltpu.SMEM)
    vmem = pl.BlockSpec(memory_space=pltpu.VMEM)
    hbm = pl.BlockSpec(memory_space=pl.ANY)
    packed = (row_devices, 3, count, width)
    return call(
        functools.partial(finish_kernel, float(total_rows)),
        shape((rows, width), BF16),
        0,
        0,
        12 * cols**3 * 3 + 2 * rows * cols * width,
        "finish",
        scratch=[
            pltpu.VMEM((cols, cols), F32),
            pltpu.VMEM((ITERS - 1, cols, cols), BF16),
            pltpu.VMEM((ITERS - 1, cols, cols), BF16),
            pltpu.VMEM((cols, width), BF16),
            pltpu.VMEM((rows, cols), BF16),
            pltpu.SemaphoreType.DMA((6,)),
        ],
        in_specs=[smem, smem, vmem, vmem] + [hbm] * 6,
    )(
        place, active, gram_mine.reshape(packed), gram_mate.reshape(packed),
        vectors, mate, across1, mate1, across2, mate2,
    )


def solution(mesh):
    in_specs = (P("row", "state"), P())
    out_specs = P("row", "state")
    return jax.shard_map(shards, mesh=mesh, in_specs=in_specs, out_specs=out_specs, check_vma=False)
```

```python
import functools

import jax
import jax.numpy as jnp
from jax import lax
from jax.experimental import pallas as pl
from jax.experimental.pallas import tpu as pltpu
from jax.sharding import PartitionSpec as P

ITERS = 5
VMEM_BYTES = 40 * 1024 * 1024
F32 = jnp.float32
BF16 = jnp.bfloat16


def dot(left, right):
    return jnp.dot(left, right, preferred_element_type=F32)


def cross(left, right):
    return lax.dot_general(left, right, (((0,), (0,)), ((), ())), preferred_element_type=F32)


def call(kernel, out_shape, n_smem, n_args, flops, name, scratch=(), in_specs=None, out_specs=None):
    smem = pl.BlockSpec(memory_space=pltpu.SMEM)
    vmem = pl.BlockSpec(memory_space=pltpu.VMEM)
    return pl.pallas_call(
        kernel,
        out_shape=out_shape,
        in_specs=in_specs or [smem] * n_smem + [vmem] * n_args,
        out_specs=out_specs or jax.tree.map(lambda _: vmem, out_shape),
        scratch_shapes=list(scratch),
        compiler_params=pltpu.CompilerParams(vmem_limit_bytes=VMEM_BYTES),
        cost_estimate=pl.CostEstimate(flops=flops, bytes_accessed=4 * 2**20, transcendentals=0),
        name=name,
    )


def chip_gram_kernel(place, own, mate, slab, later):
    chip, core = place[0], place[1]
    width = own.shape[1]
    half = later.shape[0]
    later[...] = own[pl.ds(pl.multiple_of(chip * half, half), half), :]
    slab[pl.ds(pl.multiple_of(core * width, width), width), :] = cross(own[...], own[...])
    slab[pl.ds(pl.multiple_of((1 - core) * width, width), width), :] = cross(own[...], mate[...])


def pair_gram_kernel(place, own, mate, across, chip_parts, packed):
    chip = place[0]
    half, width = across.shape
    devices, _, count, _ = packed.shape
    rows = pl.ds(pl.multiple_of(chip * half, half), half)
    same = cross(across[...], own[rows, :])
    other = cross(across[...], mate[rows, :])
    slab = jnp.concatenate([jnp.where(chip == 0, same.T, same), jnp.where(chip == 0, other.T, other)], axis=0)
    chip_sum = jnp.sum(chip_parts[...], axis=0)
    for row in range(devices):
        packed[row, 0] = chip_sum
        packed[row, 1] = slab[row * count : (row + 1) * count]


def sum_kernel(parts, total):
    total[...] = jnp.sum(parts[:, 1], axis=0)


def spread_kernel(parts, mine, theirs, across2, mate1, spread, chip_slab):
    del across2, mate1
    total = mine[...] + theirs[...]
    count = total.shape[0]
    for row in range(parts.shape[0]):
        spread[row] = total
        chip_slab[row * count : (row + 1) * count, :] = parts[row, 0]


def split(value):
    high = value.astype(BF16)
    return high, (value - high.astype(F32)).astype(BF16)


def product(left, right):
    return dot(left[0], right[0]) + (dot(left[0], right[1]) + dot(left[1], right[0]))


def row_product(left, right):
    count = left[0].shape[0]
    both = dot(jnp.concatenate(left, axis=0), right[0])
    return both[:count] + (both[count:] + dot(left[0], right[1]))


def symmetric(first, mixed, last):
    return jnp.concatenate(
        [jnp.concatenate([first, mixed], axis=1), jnp.concatenate([mixed.T, last], axis=1)], axis=0
    )


def symmetric_square(high, low):
    half = high.shape[0] // 2
    cross_part = dot(high, low)
    upper = dot(high[:half], high)
    last = dot(high[half:], high[:, half:])
    return symmetric(
        upper[:, :half] + (cross_part[:half, :half] + cross_part[:half, :half].T),
        upper[:, half:] + (cross_part[:half, half:] + cross_part[half:, :half].T),
        last + (cross_part[half:, half:] + cross_part[half:, half:].T),
    )


def symmetric_product(left, right):
    half = left[0].shape[0] // 2
    upper = product((left[0][:half], left[1][:half]), right)
    last = product((left[0][half:], left[1][half:]), (right[0][:, half:], right[1][:, half:]))
    return symmetric(upper[:, :half], upper[:, half:], last)


def finish_kernel(
    total_rows, place, chip_mine, chip_mate, other_mine, other_mate, pair_mine, pair_mate,
    own, mate, across1, mate1, across2, mate2,
    out, gram, highs, lows, factor, left, result, sems, out_sems,
):
    chip, core = place[0], place[1]
    half, width = across1.shape
    cols = gram.shape[0]
    near, far = pl.multiple_of(chip * half, half), pl.multiple_of((1 - chip) * half, half)
    copies = [
        pltpu.make_async_copy(own, left.at[:, 0:width], sems.at[0]),
        pltpu.make_async_copy(mate, left.at[:, width : 2 * width], sems.at[1]),
        pltpu.make_async_copy(across1, left.at[pl.ds(near, half), 2 * width : 3 * width], sems.at[2]),
        pltpu.make_async_copy(mate1, left.at[pl.ds(near, half), 3 * width : 4 * width], sems.at[3]),
        pltpu.make_async_copy(across2, left.at[pl.ds(far, half), 2 * width : 3 * width], sems.at[4]),
        pltpu.make_async_copy(mate2, left.at[pl.ds(far, half), 3 * width : 4 * width], sems.at[5]),
    ]
    for copy in copies:
        copy.start()

    def parts(mine, theirs):
        core0 = jnp.where(core == 0, mine, theirs)
        core1 = jnp.where(core == 0, theirs, mine)
        return core0[:width], core0[width:], core1[:width], core1[width:]

    def put(row, col, value):
        gram[row * width : (row + 1) * width, col * width : (col + 1) * width] = value

    for side in range(2):
        top0, low0, top1, low1 = parts(
            jnp.where(chip == side, chip_mine[...], other_mine[...]),
            jnp.where(chip == side, chip_mate[...], other_mate[...]),
        )
        put(2 * side, 2 * side, top0)
        put(2 * side, 2 * side + 1, low0)
        put(2 * side + 1, 2 * side, top1)
        put(2 * side + 1, 2 * side + 1, low1)
    top0, low0, top1, low1 = parts(pair_mine[...], pair_mate[...])
    off10 = jnp.where(chip == 0, low0, low1)
    off01 = jnp.where(chip == 0, low1, low0)
    put(0, 2, top0)
    put(1, 3, top1)
    put(0, 3, off01)
    put(1, 2, off10)
    put(2, 0, top0.T)
    put(3, 1, top1.T)
    put(3, 0, off01.T)
    put(2, 1, off10.T)

    states = place.shape[0] - 2
    vecs = cols // states
    col_state = lax.broadcasted_iota(jnp.int32, (1, cols), 1) // vecs
    flags = jnp.zeros((1, cols), F32)
    for state in range(states):
        flags = jnp.where(col_state == state, place[2 + state].astype(F32), flags)
    square = jnp.zeros((vecs, cols), F32)
    for state in range(states):
        rows = slice(state * vecs, (state + 1) * vecs)
        kept = jnp.where(jnp.logical_and(flags != 0, place[2 + state] != 0), gram[rows, :], 0.0)
        diagonal = lax.broadcasted_iota(jnp.int32, (vecs, cols), 0) + state * vecs == lax.broadcasted_iota(
            jnp.int32, (vecs, cols), 1
        )
        kept = kept + jnp.where(diagonal, (1.0 - flags) * total_rows, 0.0)
        gram[rows, :] = kept
        square = square + kept * kept
    frob_square = jnp.sum(jnp.sum(square, axis=0, keepdims=True), axis=1, keepdims=True)
    frob_norm = jnp.sqrt(frob_square)
    inverse_norm = 1.0 / frob_norm

    current = gram[...] * inverse_norm
    start = (2 * chip + core) * width
    last = ITERS - 2
    for step in range(last):
        high, low = split(current)
        highs[step], lows[step] = high, low
        square = symmetric_square(high, low)
        cube = symmetric_product((high, low), split(square))
        current = 2.25 * current - 1.5 * square + 0.25 * cube
    highs[last], lows[last] = split(current)
    gram[...] = current

    def times(step, slab):
        return row_product(split(slab), (highs[step], lows[step]))

    def newton(step, slab):
        return 1.5 * slab - 0.5 * times(step, slab)

    row_id = lax.broadcasted_iota(jnp.int32, (width, cols), 0) + start
    col_id = lax.broadcasted_iota(jnp.int32, (width, cols), 1)
    unit = jnp.where(row_id == col_id, 1.0, 0.0)
    slab = 1.5 * unit - 0.5 * gram[pl.ds(pl.multiple_of(start, width), width), :]
    slab = 1.5 * unit - 0.5 * times(last, newton(last, slab))
    for step in range(last, -1, -1):
        slab = newton(step, slab)
    slab = slab * jnp.sqrt(total_rows / frob_norm)

    factor[...] = jnp.where(flags != 0, slab, unit).T.astype(BF16)

    def block(index):
        return factor[pl.ds(pl.multiple_of(index * width, width), width), :]

    weights = jnp.concatenate(
        [
            block(2 * chip + core),
            block(2 * chip + 1 - core),
            block(2 * (1 - chip) + core),
            block(2 * (1 - chip) + 1 - core),
        ],
        axis=0,
    )
    for copy in copies:
        copy.wait()
    pieces = out_sems.shape[0]
    size = out.shape[0] // pieces
    stores = []
    for piece in range(pieces):
        rows = slice(piece * size, (piece + 1) * size)
        result[rows, :] = dot(left[rows, :], weights).astype(BF16)
        stores.append(pltpu.make_async_copy(result.at[rows, :], out.at[rows, :], out_sems.at[piece]))
        stores[-1].start()
    for store in stores:
        store.wait()


def shards(vectors, active):
    rows, width = vectors.shape
    half = rows // 2
    row_devices = lax.axis_size("row")
    total_rows = rows * row_devices
    cols = width * lax.axis_size("state")
    state = lax.axis_index("state")
    chip, core = state // 2, state % 2
    place = jnp.concatenate([jnp.stack([chip, core]).astype(jnp.int32), active])
    count = 2 * width // row_devices
    shape = jax.ShapeDtypeStruct
    smem = pl.BlockSpec(memory_space=pltpu.SMEM)
    vmem = pl.BlockSpec(memory_space=pltpu.VMEM)
    hbm = pl.BlockSpec(memory_space=pl.ANY)

    def swap(value, bit):
        return lax.ppermute(value, "state", [(index, index ^ bit) for index in range(4)])

    def exchange(value):
        return lax.all_to_all(value, "row", 0, 0, tiled=True)

    across1 = swap(lax.dynamic_slice_in_dim(vectors, (1 - chip) * half, half, 0), 2)
    mate = swap(vectors, 1)

    slab = shape((2 * width, width), F32)
    chip_slab, later = call(
        chip_gram_kernel, (slab, shape((half, width), BF16)), 1, 2, 4 * rows * width * width, "chip_gram"
    )(place, vectors, mate)
    chip_parts = exchange(chip_slab)
    across2 = swap(later, 2)

    packed = call(
        pair_gram_kernel, shape((row_devices, 2, count, width), F32), 1, 4, 4 * half * width * width, "pair_gram"
    )(place, vectors, mate, across1, chip_parts.reshape(row_devices, count, width))
    parts = exchange(packed.reshape(row_devices * 2 * count, width)).reshape(packed.shape)

    summed = call(sum_kernel, shape((count, width), F32), 0, 1, 0, "sum_parts")(parts)
    route = [
        (place_from * row_devices + row, (place_from ^ (2 if row < row_devices // 2 else 3)) * row_devices + row)
        for place_from in range(4)
        for row in range(row_devices)
    ]
    theirs = lax.ppermute(summed, ("state", "row"), route)
    mate1 = swap(across1, 1)
    spread, chip_mine = call(
        spread_kernel, (shape((row_devices, count, width), F32), slab), 0, 3, 0, "spread_parts",
        in_specs=[vmem, vmem, vmem, hbm, hbm],
    )(parts, summed, theirs, across2, mate1)
    pair_mine = exchange(spread.reshape(2 * width, width))
    chip_mate = swap(chip_mine, 1)
    other_mine = swap(chip_mine, 2)
    other_mate = swap(other_mine, 1)
    pair_mate = swap(pair_mine, 1)
    mate2 = swap(across2, 1)

    return call(
        functools.partial(finish_kernel, float(total_rows)),
        shape((rows, width), BF16),
        0,
        0,
        12 * cols**3 * 3 + 2 * rows * cols * width,
        "finish",
        scratch=[
            pltpu.VMEM((cols, cols), F32),
            pltpu.VMEM((ITERS - 1, cols, cols), BF16),
            pltpu.VMEM((ITERS - 1, cols, cols), BF16),
            pltpu.VMEM((cols, width), BF16),
            pltpu.VMEM((rows, cols), BF16),
            pltpu.VMEM((rows, width), BF16),
            pltpu.SemaphoreType.DMA((6,)),
            pltpu.SemaphoreType.DMA((4,)),
        ],
        in_specs=[smem] + [vmem] * 6 + [hbm] * 6,
        out_specs=hbm,
    )(
        place, chip_mine, chip_mate, other_mine, other_mate, pair_mine, pair_mate,
        vectors, mate, across1, mate1, across2, mate2,
    )


def solution(mesh):
    in_specs = (P("row", "state"), P())
    out_specs = P("row", "state")
    return jax.shard_map(shards, mesh=mesh, in_specs=in_specs, out_specs=out_specs, check_vma=False)
```

```python
import functools

import jax
import jax.numpy as jnp
from jax import lax
from jax.experimental import pallas as pl
from jax.experimental.pallas import tpu as pltpu
from jax.sharding import PartitionSpec as P

ITERS = 5
F32 = jnp.float32
BF16 = jnp.bfloat16
SMEM = pl.BlockSpec(memory_space=pltpu.SMEM)
VMEM = pl.BlockSpec(memory_space=pltpu.VMEM)
ANY = pl.BlockSpec(memory_space=pl.ANY)


def dot(left, right):
    return jnp.dot(left, right, preferred_element_type=F32)


def cross(left, right):
    return lax.dot_general(left, right, (((0,), (0,)), ((), ())), preferred_element_type=F32)


def call(kernel, out_shape, n_smem, n_args, flops, name, scratch=(), in_specs=None, out_specs=None, mib=12, aliases=None):
    return pl.pallas_call(
        kernel,
        out_shape=out_shape,
        in_specs=in_specs or [SMEM] * n_smem + [VMEM] * n_args,
        out_specs=out_specs or jax.tree.map(lambda _: VMEM, out_shape),
        scratch_shapes=list(scratch),
        input_output_aliases=aliases or {},
        compiler_params=pltpu.CompilerParams(vmem_limit_bytes=mib * 2**20),
        cost_estimate=pl.CostEstimate(flops=flops, bytes_accessed=2**20, transcendentals=0),
        name=name,
    )


def piece(place, step, size):
    return pl.ds(pl.multiple_of(lax.bitwise_xor(place[2], jnp.int32(step)) * size, size), size)


def tree_sum(values):
    while len(values) > 1:
        values = [left + right for left, right in zip(values[::2], values[1::2])]
    return values[0]


def later_kernel(place, own, after, part, sem):
    del after
    size = part.shape[0]
    copy = pltpu.make_async_copy(own.at[pl.ds(pl.multiple_of(place[0] * size, size), size), :], part, sem)
    copy.start()
    copy.wait()


def chip_gram_kernel(place, own, mate, keep, send1, send2, send3, slab):
    core = place[1]
    width = own.shape[1]
    size = keep.shape[0]
    slab[pl.ds(pl.multiple_of(core * width, width), width), :] = cross(own[...], own[...])
    slab[pl.ds(pl.multiple_of((1 - core) * width, width), width), :] = cross(own[...], mate[...])
    for step, out in enumerate((keep, send1, send2, send3)):
        out[...] = slab[piece(place, step, size), :]


def chip_sum_kernel(keep, part1, part2, part3, later, total):
    del later
    total[...] = tree_sum([keep[...], part1[...], part2[...], part3[...]])


def pair_gram_kernel(place, own, mate, across, *rest):
    chip_parts, (chip_piece, keep, send1, send2, send3, slab) = rest[:-6], rest[-6:]
    chip = place[0]
    half, width = across.shape
    size = keep.shape[0]
    rows = pl.ds(pl.multiple_of(chip * half, half), half)
    same = cross(across[...], own[rows, :])
    other = cross(across[...], mate[rows, :])
    slab[0:width, :] = jnp.where(chip == 0, same.T, same)
    slab[width : 2 * width, :] = jnp.where(chip == 0, other.T, other)
    chip_sum = tree_sum([part[...] for part in chip_parts])
    chip_piece[...] = chip_sum
    keep[...] = slab[piece(place, 0, size), :]
    for step, out in enumerate((send1, send2, send3)):
        out[0:size, :] = slab[piece(place, step + 1, size), :]
        out[size : 2 * size, :] = chip_sum


def pass_kernel(value, after, same):
    del value, after, same


def group_sum_kernel(place, keep, chip_piece, part1, part2, part3, mate1, total, payload, chip_slab):
    del mate1
    size = keep.shape[0]
    parts = (part1, part2, part3)
    group_sum = tree_sum([keep[...]] + [part[0:size, :] for part in parts])
    total[...] = group_sum
    payload[0:size, :] = group_sum
    payload[size : 2 * size, :] = chip_piece[...]
    chip_slab[piece(place, 0, size), :] = chip_piece[...]
    for step, part in enumerate(parts):
        chip_slab[piece(place, step + 1, size), :] = part[size : 2 * size, :]


def pair_sum_kernel(total, across, *rest):
    parts, payload = rest[:-2], rest[-1]
    size = total.shape[0]
    payload[0:size, :] = tree_sum([total[...], across[0:size, :]] + [part[...] for part in parts])
    payload[size : 2 * size, :] = across[size : 2 * size, :]


def join_kernel(place, own, part1, part2, part3, chip_mine, joined):
    size = own.shape[0] // 2
    for step, part in enumerate((own, part1, part2, part3)):
        joined[piece(place, step, size), :] = part[0:size, :]
        start = pl.multiple_of(8 * size + lax.bitwise_xor(place[2], jnp.int32(step)) * size, size)
        joined[pl.ds(start, size), :] = part[size : 2 * size, :]
    joined[4 * size : 8 * size, :] = chip_mine[...]


def split(value):
    high = value.astype(BF16)
    return high, (value - high.astype(F32)).astype(BF16)


def product(left, right):
    return dot(left[0], right[0]) + (dot(left[0], right[1]) + dot(left[1], right[0]))


def row_product(left, right):
    count = left[0].shape[0]
    both = dot(jnp.concatenate(left, axis=0), right[0])
    return both[:count] + (both[count:] + dot(left[0], right[1]))


def symmetric(first, mixed, last):
    return jnp.concatenate(
        [jnp.concatenate([first, mixed], axis=1), jnp.concatenate([mixed.T, last], axis=1)], axis=0
    )


def symmetric_square(high, low):
    half = high.shape[0] // 2
    cross_part = dot(high, low)
    upper = dot(high[:half], high)
    last = dot(high[half:], high[:, half:])
    return symmetric(
        upper[:, :half] + (cross_part[:half, :half] + cross_part[:half, :half].T),
        upper[:, half:] + (cross_part[:half, half:] + cross_part[half:, :half].T),
        last + (cross_part[half:, half:] + cross_part[half:, half:].T),
    )


def symmetric_product(left, right):
    half = left[0].shape[0] // 2
    upper = product((left[0][:half], left[1][:half]), right)
    last = product((left[0][half:], left[1][half:]), (right[0][:, half:], right[1][:, half:]))
    return symmetric(upper[:, :half], upper[:, half:], last)


def finish_kernel(
    total_rows, place, active, joined_mine, joined_mate, own, mate, across1, mate1, across2, mate2,
    out, gram, highs, lows, factor, left, result, state_flags, sems, out_sems,
):
    chip, core = place[0], place[1]
    half, width = across1.shape
    cols = gram.shape[0]
    near, far = pl.multiple_of(chip * half, half), pl.multiple_of((1 - chip) * half, half)
    fetch = pltpu.make_async_copy(active, state_flags, sems.at[6])
    fetch.start()
    every = pl.ds(0, 2 * half)
    copies = [
        pltpu.make_async_copy(source, left.at[where, index * width : (index + 1) * width], sems.at[number])
        for number, (source, where, index) in enumerate(
            [
                (own, every, 0),
                (mate, every, 1),
                (across1, pl.ds(near, half), 2),
                (mate1, pl.ds(near, half), 3),
                (across2, pl.ds(far, half), 2),
                (mate2, pl.ds(far, half), 3),
            ]
        )
    ]
    for copy in copies:
        copy.start()

    def parts(part):
        rows = slice(2 * width * part, 2 * width * (part + 1))
        mine, theirs = joined_mine[rows, :], joined_mate[rows, :]
        core0 = jnp.where(core == 0, mine, theirs)
        core1 = jnp.where(core == 0, theirs, mine)
        return core0[:width], core0[width:], core1[:width], core1[width:]

    def put(row, col, value):
        gram[row * width : (row + 1) * width, col * width : (col + 1) * width] = value

    here, there = parts(1), parts(2)
    there = there[0], there[3], there[2], there[1]
    for side in range(2):
        top0, low0, top1, low1 = [jnp.where(chip == side, near_part, far_part) for near_part, far_part in zip(here, there)]
        put(2 * side, 2 * side, top0)
        put(2 * side, 2 * side + 1, low0)
        put(2 * side + 1, 2 * side, top1)
        put(2 * side + 1, 2 * side + 1, low1)
    top0, low0, top1, low1 = parts(0)
    off10 = jnp.where(chip == 0, low0, low1)
    off01 = jnp.where(chip == 0, low1, low0)
    put(0, 2, top0)
    put(1, 3, top1)
    put(0, 3, off01)
    put(1, 2, off10)
    put(2, 0, top0.T)
    put(3, 1, top1.T)
    put(3, 0, off01.T)
    put(2, 1, off10.T)

    fetch.wait()
    states = active.shape[0]
    vecs = cols // states
    col_state = lax.broadcasted_iota(jnp.int32, (1, cols), 1) // vecs
    flags = jnp.zeros((1, cols), F32)
    for state in range(states):
        flags = jnp.where(col_state == state, state_flags[state].astype(F32), flags)
    square = jnp.zeros((vecs, cols), F32)
    for state in range(states):
        rows = slice(state * vecs, (state + 1) * vecs)
        kept = jnp.where(jnp.logical_and(flags != 0, state_flags[state] != 0), gram[rows, :], 0.0)
        diagonal = lax.broadcasted_iota(jnp.int32, (vecs, cols), 0) + state * vecs == lax.broadcasted_iota(
            jnp.int32, (vecs, cols), 1
        )
        kept = kept + jnp.where(diagonal, (1.0 - flags) * total_rows, 0.0)
        gram[rows, :] = kept
        square = square + kept * kept
    frob_square = jnp.sum(jnp.sum(square, axis=0, keepdims=True), axis=1, keepdims=True)
    frob_norm = jnp.sqrt(frob_square)
    inverse_norm = 1.0 / frob_norm

    current = gram[...] * inverse_norm
    start = (2 * chip + core) * width
    last = ITERS - 2
    for step in range(last):
        high, low = split(current)
        highs[step], lows[step] = high, low
        square = symmetric_square(high, low)
        cube = symmetric_product((high, low), split(square))
        current = 2.25 * current - 1.5 * square + 0.25 * cube
    highs[last], lows[last] = split(current)
    gram[...] = current

    def times(step, slab):
        return row_product(split(slab), (highs[step], lows[step]))

    def newton(step, slab):
        return 1.5 * slab - 0.5 * times(step, slab)

    row_id = lax.broadcasted_iota(jnp.int32, (width, cols), 0) + start
    col_id = lax.broadcasted_iota(jnp.int32, (width, cols), 1)
    unit = jnp.where(row_id == col_id, 1.0, 0.0)
    slab = 1.5 * unit - 0.5 * gram[pl.ds(pl.multiple_of(start, width), width), :]
    slab = 1.5 * unit - 0.5 * times(last, newton(last, slab))
    for step in range(last, -1, -1):
        slab = newton(step, slab)
    slab = slab * jnp.sqrt(total_rows / frob_norm)

    factor[...] = jnp.where(flags != 0, slab, unit).T.astype(BF16)

    def block(index):
        return factor[pl.ds(pl.multiple_of(index * width, width), width), :]

    weights = jnp.concatenate(
        [
            block(2 * chip + core),
            block(2 * chip + 1 - core),
            block(2 * (1 - chip) + core),
            block(2 * (1 - chip) + 1 - core),
        ],
        axis=0,
    )
    for copy in copies:
        copy.wait()
    pieces = out_sems.shape[0]
    size = out.shape[0] // pieces
    stores = []
    for piece in range(pieces):
        rows = slice(piece * size, (piece + 1) * size)
        result[rows, :] = dot(left[rows, :], weights).astype(BF16)
        stores.append(pltpu.make_async_copy(result.at[rows, :], out.at[rows, :], out_sems.at[piece]))
        stores[-1].start()
    for store in stores:
        store.wait()


def shards(vectors, active):
    rows, width = vectors.shape
    half = rows // 2
    row_devices = lax.axis_size("row")
    total_rows = rows * row_devices
    cols = width * lax.axis_size("state")
    state, row = lax.axis_index("state"), lax.axis_index("row")
    chip, core = state // 2, state % 2
    place = jnp.stack([chip, core, row % 4]).astype(jnp.int32)
    size = width // 2
    shape = jax.ShapeDtypeStruct
    small, slab = shape((size, width), F32), shape((2 * width, width), F32)

    def swap(value, bit):
        return lax.ppermute(value, "state", [(index, index ^ bit) for index in range(4)])

    def move(value, bits, chips=0):
        pairs = []
        for state_from in range(4):
            for row_from in range(row_devices):
                state_to = state_from ^ ((2 if row_from % 4 < 2 else 3) if chips else 0)
                pairs.append((state_from * row_devices + row_from, state_to * row_devices + (row_from ^ bits)))
        return lax.ppermute(value, ("state", "row"), pairs)

    def after(value, other):
        return call(
            pass_kernel, shape(value.shape, value.dtype), 0, 0, 0, "after", in_specs=[ANY, ANY], out_specs=ANY,
            aliases={0: 0},
        )(value, other)

    across1 = swap(lax.dynamic_slice_in_dim(vectors, (1 - chip) * half, half, 0), 2)
    mate = swap(vectors, 1)
    keep, *sends = call(
        chip_gram_kernel, (small,) * 4, 1, 2, 4 * rows * width * width, "chip_gram", scratch=[pltpu.VMEM(slab.shape, F32)]
    )(place, vectors, mate)
    later = call(
        later_kernel, shape((half, width), BF16), 1, 0, 0, "later", scratch=[pltpu.SemaphoreType.DMA],
        in_specs=[SMEM, ANY, ANY], out_specs=ANY,
    )(place, vectors, keep)
    across2 = swap(later, 2)

    groups = [4 * index for index in range(row_devices // 4)]
    parts = [move(send, step + 1) for step, send in enumerate(sends)]
    chip_sum = call(chip_sum_kernel, small, 0, 4, 0, "chip_sum", in_specs=[VMEM] * 4 + [ANY])(keep, *parts, later)
    chip_parts = [chip_sum] + [move(chip_sum, bits) for bits in groups[1:]]
    double = shape((2 * size, width), F32)
    chip_piece, keep, *sends = call(
        pair_gram_kernel, (small, small, double, double, double), 1, 3 + len(chip_parts), 4 * half * width * width,
        "pair_gram", scratch=[pltpu.VMEM(slab.shape, F32)],
    )(place, vectors, mate, across1, *chip_parts)
    parts = [move(send, step + 1) for step, send in enumerate(sends)]
    mate1 = swap(after(across1, chip_piece), 1)
    pair_sum, payload, chip_mine = call(
        group_sum_kernel, (small, double, slab), 0, 0, 0, "group_sum", in_specs=[SMEM] + [VMEM] * 5 + [ANY]
    )(place, keep, chip_piece, *parts, mate1)
    pair_parts = [move(payload, 0, 1)] + [move(pair_sum, bits, chips) for bits in groups[1:] for chips in range(2)]
    payload = call(
        pair_sum_kernel, double, 0, 0, 0, "pair_sum", in_specs=[VMEM] * (1 + len(pair_parts)) + [ANY]
    )(pair_sum, *pair_parts, across2)
    parts = [move(payload, step) for step in (1, 2, 3)]
    mate2 = swap(after(across2, payload), 1)
    joined_mine = call(join_kernel, shape((6 * width, width), F32), 1, 5, 0, "join")(place, payload, *parts, chip_mine)
    joined_mate = swap(joined_mine, 1)

    return call(
        functools.partial(finish_kernel, float(total_rows)),
        shape((rows, width), BF16),
        0,
        0,
        12 * cols**3 * 3 + 2 * rows * cols * width,
        "finish",
        scratch=[
            pltpu.VMEM((cols, cols), F32),
            pltpu.VMEM((ITERS - 1, cols, cols), BF16),
            pltpu.VMEM((ITERS - 1, cols, cols), BF16),
            pltpu.VMEM((cols, width), BF16),
            pltpu.VMEM((rows, cols), BF16),
            pltpu.VMEM((rows, width), BF16),
            pltpu.SMEM(active.shape, jnp.int32),
            pltpu.SemaphoreType.DMA((7,)),
            pltpu.SemaphoreType.DMA((4,)),
        ],
        in_specs=[SMEM, ANY, VMEM, VMEM] + [ANY] * 6,
        out_specs=ANY,
        mib=24,
    )(
        place, active, joined_mine, joined_mate, vectors, mate, across1, mate1, across2, mate2
    )


def solution(mesh):
    in_specs = (P("row", "state"), P())
    out_specs = P("row", "state")
    return jax.shard_map(shards, mesh=mesh, in_specs=in_specs, out_specs=out_specs, check_vma=False)
```

```python
import functools

import jax
import jax.numpy as jnp
from jax import lax
from jax.experimental import pallas as pl
from jax.experimental.pallas import tpu as pltpu
from jax.sharding import PartitionSpec as P

ITERS = 5
F32 = jnp.float32
BF16 = jnp.bfloat16
VMEM = pl.BlockSpec(memory_space=pltpu.VMEM)
ANY = pl.BlockSpec(memory_space=pl.ANY)


def dot(left, right):
    return jnp.dot(left, right, preferred_element_type=F32)


def cross(left, right):
    return lax.dot_general(left, right, (((0,), (0,)), ((), ())), preferred_element_type=F32)


def call(kernel, out_shape, n_args, flops, name, scratch=(), in_specs=None, out_specs=None, mib=12, aliases=None):
    return pl.pallas_call(
        kernel,
        out_shape=out_shape,
        in_specs=in_specs or [VMEM] * n_args,
        out_specs=out_specs or jax.tree.map(lambda _: VMEM, out_shape),
        scratch_shapes=list(scratch),
        input_output_aliases=aliases or {},
        compiler_params=pltpu.CompilerParams(vmem_limit_bytes=mib * 2**20),
        cost_estimate=pl.CostEstimate(flops=0, bytes_accessed=0, transcendentals=0),
        name=name,
    )


def chip_index():
    return lax.axis_index("state") // 2


def core_index():
    return lax.axis_index("state") % 2


def piece(step, size, base=0):
    member = lax.bitwise_xor(lax.axis_index("row") % 4, jnp.int32(step))
    return pl.ds(pl.multiple_of(base + member * size, size), size)


def tree_sum(values):
    while len(values) > 1:
        values = [left + right for left, right in zip(values[::2], values[1::2])]
    return values[0]


def later_kernel(own, after, part, sem):
    del after
    size = part.shape[0]
    copy = pltpu.make_async_copy(own.at[pl.ds(pl.multiple_of(chip_index() * size, size), size), :], part, sem)
    copy.start()
    copy.wait()


def chip_gram_kernel(own, mate, keep, send1, send2, send3, slab):
    core = core_index()
    width = own.shape[1]
    size = keep.shape[0]
    slab[pl.ds(pl.multiple_of(core * width, width), width), :] = cross(own[...], own[...])
    slab[pl.ds(pl.multiple_of((1 - core) * width, width), width), :] = cross(own[...], mate[...])
    for step, out in enumerate((keep, send1, send2, send3)):
        out[...] = slab[piece(step, size), :]


def chip_sum_kernel(keep, part1, part2, part3, later, total):
    del later
    total[...] = tree_sum([keep[...], part1[...], part2[...], part3[...]])


def pair_gram_kernel(own, mate, across, *rest):
    chip_parts, (chip_piece, keep, send1, send2, send3, slab) = rest[:-6], rest[-6:]
    chip = chip_index()
    half, width = across.shape
    size = keep.shape[0]
    rows = pl.ds(pl.multiple_of(chip * half, half), half)
    same = cross(across[...], own[rows, :])
    other = cross(across[...], mate[rows, :])
    slab[0:width, :] = jnp.where(chip == 0, same.T, same)
    slab[width : 2 * width, :] = jnp.where(chip == 0, other.T, other)
    chip_sum = tree_sum([part[...] for part in chip_parts])
    chip_piece[...] = chip_sum
    keep[...] = slab[piece(0, size), :]
    for step, out in enumerate((send1, send2, send3)):
        out[0:size, :] = slab[piece(step + 1, size), :]
        out[size : 2 * size, :] = chip_sum


def pass_kernel(value, after, same):
    del value, after, same


def group_sum_kernel(keep, chip_piece, part1, part2, part3, mate1, total, payload, chip_slab):
    del mate1
    size = keep.shape[0]
    parts = (part1, part2, part3)
    group_sum = tree_sum([keep[...]] + [part[0:size, :] for part in parts])
    total[...] = group_sum
    payload[0:size, :] = group_sum
    payload[size : 2 * size, :] = chip_piece[...]
    chip_slab[piece(0, size), :] = chip_piece[...]
    for step, part in enumerate(parts):
        chip_slab[piece(step + 1, size), :] = part[size : 2 * size, :]


def pair_sum_kernel(total, across, *rest):
    parts, payload = rest[:-2], rest[-1]
    size = total.shape[0]
    payload[0:size, :] = tree_sum([total[...], across[0:size, :]] + [part[...] for part in parts])
    payload[size : 2 * size, :] = across[size : 2 * size, :]


def join_kernel(own, part1, part2, part3, chip_mine, joined):
    size = own.shape[0] // 2
    for step, part in enumerate((own, part1, part2, part3)):
        joined[piece(step, size), :] = part[0:size, :]
        joined[piece(step, size, 8 * size), :] = part[size : 2 * size, :]
    joined[4 * size : 8 * size, :] = chip_mine[...]


def split(value):
    high = value.astype(BF16)
    return high, (value - high.astype(F32)).astype(BF16)


def product(left, right):
    return dot(left[0], right[0]) + (dot(left[0], right[1]) + dot(left[1], right[0]))


def row_product(left, right):
    count = left[0].shape[0]
    both = dot(jnp.concatenate(left, axis=0), right[0])
    return both[:count] + (both[count:] + dot(left[0], right[1]))


def symmetric(first, mixed, last):
    return jnp.concatenate(
        [jnp.concatenate([first, mixed], axis=1), jnp.concatenate([mixed.T, last], axis=1)], axis=0
    )


def symmetric_square(high, low):
    half = high.shape[0] // 2
    cross_part = dot(high, low)
    upper = dot(high[:half], high)
    last = dot(high[half:], high[:, half:])
    return symmetric(
        upper[:, :half] + (cross_part[:half, :half] + cross_part[:half, :half].T),
        upper[:, half:] + (cross_part[:half, half:] + cross_part[half:, :half].T),
        last + (cross_part[half:, half:] + cross_part[half:, half:].T),
    )


def symmetric_product(left, right):
    half = left[0].shape[0] // 2
    upper = product((left[0][:half], left[1][:half]), right)
    last = product((left[0][half:], left[1][half:]), (right[0][:, half:], right[1][:, half:]))
    return symmetric(upper[:, :half], upper[:, half:], last)


def finish_kernel(
    total_rows, active, joined_mine, joined_mate, own, mate, across1, mate1, across2, mate2,
    out, gram, highs, lows, factor, left, result, state_flags, sems, out_sems,
):
    chip, core = chip_index(), core_index()
    half, width = across1.shape
    cols = gram.shape[0]
    near, far = pl.multiple_of(chip * half, half), pl.multiple_of((1 - chip) * half, half)
    fetch = pltpu.make_async_copy(active, state_flags, sems.at[6])
    fetch.start()
    every = pl.ds(0, 2 * half)
    copies = [
        pltpu.make_async_copy(source, left.at[where, index * width : (index + 1) * width], sems.at[number])
        for number, (source, where, index) in enumerate(
            [
                (own, every, 0),
                (mate, every, 1),
                (across1, pl.ds(near, half), 2),
                (mate1, pl.ds(near, half), 3),
                (across2, pl.ds(far, half), 2),
                (mate2, pl.ds(far, half), 3),
            ]
        )
    ]
    for copy in copies:
        copy.start()

    def parts(part):
        rows = slice(2 * width * part, 2 * width * (part + 1))
        mine, theirs = joined_mine[rows, :], joined_mate[rows, :]
        core0 = jnp.where(core == 0, mine, theirs)
        core1 = jnp.where(core == 0, theirs, mine)
        return core0[:width], core0[width:], core1[:width], core1[width:]

    def put(row, col, value):
        gram[row * width : (row + 1) * width, col * width : (col + 1) * width] = value

    here, there = parts(1), parts(2)
    there = there[0], there[3], there[2], there[1]
    for side in range(2):
        top0, low0, top1, low1 = [jnp.where(chip == side, near_part, far_part) for near_part, far_part in zip(here, there)]
        put(2 * side, 2 * side, top0)
        put(2 * side, 2 * side + 1, low0)
        put(2 * side + 1, 2 * side, top1)
        put(2 * side + 1, 2 * side + 1, low1)
    top0, low0, top1, low1 = parts(0)
    off10 = jnp.where(chip == 0, low0, low1)
    off01 = jnp.where(chip == 0, low1, low0)
    put(0, 2, top0)
    put(1, 3, top1)
    put(0, 3, off01)
    put(1, 2, off10)
    put(2, 0, top0.T)
    put(3, 1, top1.T)
    put(3, 0, off01.T)
    put(2, 1, off10.T)

    fetch.wait()
    states = active.shape[0]
    vecs = cols // states
    col_state = lax.broadcasted_iota(jnp.int32, (1, cols), 1) // vecs
    flags = jnp.zeros((1, cols), F32)
    for state in range(states):
        flags = jnp.where(col_state == state, state_flags[state].astype(F32), flags)
    square = jnp.zeros((vecs, cols), F32)
    for state in range(states):
        rows = slice(state * vecs, (state + 1) * vecs)
        kept = jnp.where(jnp.logical_and(flags != 0, state_flags[state] != 0), gram[rows, :], 0.0)
        diagonal = lax.broadcasted_iota(jnp.int32, (vecs, cols), 0) + state * vecs == lax.broadcasted_iota(
            jnp.int32, (vecs, cols), 1
        )
        kept = kept + jnp.where(diagonal, (1.0 - flags) * total_rows, 0.0)
        gram[rows, :] = kept
        square = square + kept * kept
    frob_square = jnp.sum(jnp.sum(square, axis=0, keepdims=True), axis=1, keepdims=True)
    frob_norm = jnp.sqrt(frob_square)
    inverse_norm = 1.0 / frob_norm

    current = gram[...] * inverse_norm
    start = (2 * chip + core) * width
    last = ITERS - 2
    for step in range(last):
        high, low = split(current)
        highs[step], lows[step] = high, low
        square = symmetric_square(high, low)
        cube = symmetric_product((high, low), split(square))
        current = 2.25 * current - 1.5 * square + 0.25 * cube
    highs[last], lows[last] = split(current)
    gram[...] = current

    def times(step, slab):
        return row_product(split(slab), (highs[step], lows[step]))

    def newton(step, slab):
        return 1.5 * slab - 0.5 * times(step, slab)

    row_id = lax.broadcasted_iota(jnp.int32, (width, cols), 0) + start
    col_id = lax.broadcasted_iota(jnp.int32, (width, cols), 1)
    unit = jnp.where(row_id == col_id, 1.0, 0.0)
    slab = 1.5 * unit - 0.5 * gram[pl.ds(pl.multiple_of(start, width), width), :]
    slab = 1.5 * unit - 0.5 * times(last, newton(last, slab))
    for step in range(last, -1, -1):
        slab = newton(step, slab)
    slab = slab * jnp.sqrt(total_rows / frob_norm)

    factor[...] = jnp.where(flags != 0, slab, unit).T.astype(BF16)

    def block(index):
        return factor[pl.ds(pl.multiple_of(index * width, width), width), :]

    weights = jnp.concatenate(
        [
            block(2 * chip + core),
            block(2 * chip + 1 - core),
            block(2 * (1 - chip) + core),
            block(2 * (1 - chip) + 1 - core),
        ],
        axis=0,
    )
    for copy in copies:
        copy.wait()
    pieces = out_sems.shape[0]
    size = out.shape[0] // pieces
    stores = []
    for piece in range(pieces):
        rows = slice(piece * size, (piece + 1) * size)
        result[rows, :] = dot(left[rows, :], weights).astype(BF16)
        stores.append(pltpu.make_async_copy(result.at[rows, :], out.at[rows, :], out_sems.at[piece]))
        stores[-1].start()
    for store in stores:
        store.wait()


def shards(vectors, active):
    rows, width = vectors.shape
    half = rows // 2
    row_devices = lax.axis_size("row")
    total_rows = rows * row_devices
    cols = width * lax.axis_size("state")
    chip = chip_index()
    size = width // 2
    shape = jax.ShapeDtypeStruct
    small, slab = shape((size, width), F32), shape((2 * width, width), F32)

    def swap(value, bit):
        return lax.ppermute(value, "state", [(index, index ^ bit) for index in range(4)])

    def move(value, bits, chips=0):
        pairs = []
        for state_from in range(4):
            for row_from in range(row_devices):
                state_to = state_from ^ ((2 if row_from % 4 < 2 else 3) if chips else 0)
                pairs.append((state_from * row_devices + row_from, state_to * row_devices + (row_from ^ bits)))
        return lax.ppermute(value, ("state", "row"), pairs)

    def after(value, other):
        return call(
            pass_kernel, shape(value.shape, value.dtype), 0, 0, "after", in_specs=[ANY, ANY], out_specs=ANY,
            aliases={0: 0},
        )(value, other)

    across1 = swap(lax.dynamic_slice_in_dim(vectors, (1 - chip) * half, half, 0), 2)
    mate = swap(vectors, 1)
    keep, *sends = call(
        chip_gram_kernel, (small,) * 4, 2, 4 * rows * width * width, "chip_gram", scratch=[pltpu.VMEM(slab.shape, F32)]
    )(vectors, mate)
    later = call(
        later_kernel, shape((half, width), BF16), 0, 0, "later", scratch=[pltpu.SemaphoreType.DMA],
        in_specs=[ANY, ANY], out_specs=ANY,
    )(vectors, keep)
    across2 = swap(later, 2)

    groups = [4 * index for index in range(row_devices // 4)]
    parts = [move(send, step + 1) for step, send in enumerate(sends)]
    chip_sum = call(chip_sum_kernel, small, 4, 0, "chip_sum", in_specs=[VMEM] * 4 + [ANY])(keep, *parts, later)
    chip_parts = [chip_sum] + [move(chip_sum, bits) for bits in groups[1:]]
    double = shape((2 * size, width), F32)
    chip_piece, keep, *sends = call(
        pair_gram_kernel, (small, small, double, double, double), 3 + len(chip_parts), 4 * half * width * width,
        "pair_gram", scratch=[pltpu.VMEM(slab.shape, F32)],
    )(vectors, mate, across1, *chip_parts)
    parts = [move(send, step + 1) for step, send in enumerate(sends)]
    mate1 = swap(after(across1, chip_piece), 1)
    pair_sum, payload, chip_mine = call(
        group_sum_kernel, (small, double, slab), 0, 0, "group_sum", in_specs=[VMEM] * 5 + [ANY]
    )(keep, chip_piece, *parts, mate1)
    pair_parts = [move(payload, 0, 1)] + [move(pair_sum, bits, chips) for bits in groups[1:] for chips in range(2)]
    payload = call(
        pair_sum_kernel, double, 0, 0, "pair_sum", in_specs=[VMEM] * (1 + len(pair_parts)) + [ANY]
    )(pair_sum, *pair_parts, across2)
    parts = [move(payload, step) for step in (1, 2, 3)]
    mate2 = swap(after(across2, payload), 1)
    joined_mine = call(join_kernel, shape((6 * width, width), F32), 5, 0, "join")(payload, *parts, chip_mine)
    joined_mate = swap(joined_mine, 1)

    return call(
        functools.partial(finish_kernel, float(total_rows)),
        shape((rows, width), BF16),
        0,
        12 * cols**3 * 3 + 2 * rows * cols * width,
        "finish",
        scratch=[
            pltpu.VMEM((cols, cols), F32),
            pltpu.VMEM((ITERS - 1, cols, cols), BF16),
            pltpu.VMEM((ITERS - 1, cols, cols), BF16),
            pltpu.VMEM((cols, width), BF16),
            pltpu.VMEM((rows, cols), BF16),
            pltpu.VMEM((rows, width), BF16),
            pltpu.SMEM(active.shape, jnp.int32),
            pltpu.SemaphoreType.DMA((7,)),
            pltpu.SemaphoreType.DMA((4,)),
        ],
        in_specs=[ANY, VMEM, VMEM] + [ANY] * 6,
        out_specs=ANY,
        mib=24,
    )(
        active, joined_mine, joined_mate, vectors, mate, across1, mate1, across2, mate2
    )


def solution(mesh):
    in_specs = (P("row", "state"), P())
    out_specs = P("row", "state")
    return jax.shard_map(shards, mesh=mesh, in_specs=in_specs, out_specs=out_specs, check_vma=False)
```

```python
import functools

import jax
import jax.numpy as jnp
from jax import lax
from jax.experimental import pallas as pl
from jax.experimental.pallas import tpu as pltpu
from jax.sharding import PartitionSpec as P

ITERS = 5
F32 = jnp.float32
BF16 = jnp.bfloat16
VMEM = pl.BlockSpec(memory_space=pltpu.VMEM)
ANY = pl.BlockSpec(memory_space=pl.ANY)


def dot(left, right):
    return jnp.dot(left, right, preferred_element_type=F32)


def cross(left, right):
    return lax.dot_general(left, right, (((0,), (0,)), ((), ())), preferred_element_type=F32)


def call(kernel, out_shape, n_args, flops, name, scratch=(), in_specs=None, out_specs=None, mib=12, aliases=None):
    return pl.pallas_call(
        kernel,
        out_shape=out_shape,
        in_specs=in_specs or [VMEM] * n_args,
        out_specs=out_specs or jax.tree.map(lambda _: VMEM, out_shape),
        scratch_shapes=list(scratch),
        input_output_aliases=aliases or {},
        compiler_params=pltpu.CompilerParams(vmem_limit_bytes=mib * 2**20),
        cost_estimate=pl.CostEstimate(flops=0, bytes_accessed=0, transcendentals=0),
        name=name,
    )


def chip_index():
    return lax.axis_index("state") // 2


def core_index():
    return lax.axis_index("state") % 2


def piece(step, size, base=0):
    member = lax.bitwise_xor(lax.axis_index("row") % 4, jnp.int32(step))
    return pl.ds(pl.multiple_of(base + member * size, size), size)


def tree_sum(values):
    while len(values) > 1:
        values = [left + right for left, right in zip(values[::2], values[1::2])]
    return values[0]


def later_kernel(own, after, part, sem):
    del after
    size = part.shape[0]
    copy = pltpu.make_async_copy(own.at[pl.ds(pl.multiple_of(chip_index() * size, size), size), :], part, sem)
    copy.start()
    copy.wait()


def chip_gram_kernel(own, mate, keep, send1, send2, send3, slab):
    core = core_index()
    width = own.shape[1]
    size = keep.shape[0]
    between = cross(own[...], mate[...])
    slab[0:width, :] = cross(own[...], own[...])
    slab[width:, :] = jnp.where(core == 0, between[: width // 2, :], between.T[width // 2 :, :])
    for step, out in enumerate((keep, send1, send2, send3)):
        out[...] = slab[piece(step, size), :]


def chip_sum_kernel(keep, part1, part2, part3, later, total):
    del later
    total[...] = tree_sum([keep[...], part1[...], part2[...], part3[...]])


def pair_gram_kernel(own, mate, across, *rest):
    chip_parts, (chip_piece, keep, send1, send2, send3, slab) = rest[:-6], rest[-6:]
    chip = chip_index()
    half, width = across.shape
    size = keep.shape[0]
    rows = pl.ds(pl.multiple_of(chip * half, half), half)
    same = cross(across[...], own[rows, :])
    other = cross(across[...], mate[rows, :])
    slab[0:width, :] = jnp.where(chip == 0, same.T, same)
    slab[width : 2 * width, :] = jnp.where(chip == 0, other.T, other)
    chip_sum = tree_sum([part[...] for part in chip_parts])
    chip_piece[...] = chip_sum
    keep[...] = slab[piece(0, size), :]
    for step, out in enumerate((send1, send2, send3)):
        out[0:size, :] = slab[piece(step + 1, size), :]
        out[size:, :] = chip_sum


def pass_kernel(value, after, same):
    del value, after, same


def group_sum_kernel(keep, chip_piece, part1, part2, part3, total, payload, chip_slab):
    size, count = keep.shape[0], chip_piece.shape[0]
    parts = (part1, part2, part3)
    group_sum = tree_sum([keep[...]] + [part[0:size, :] for part in parts])
    total[...] = group_sum
    payload[0:size, :] = group_sum
    payload[size:, :] = chip_piece[...]
    chip_slab[piece(0, count), :] = chip_piece[...]
    for step, part in enumerate(parts):
        chip_slab[piece(step + 1, count), :] = part[size:, :]


def pair_sum_kernel(total, across, *rest):
    parts, pieces = rest[:-1], rest[-1]
    size = total.shape[0]
    pieces[0:size, :] = tree_sum([total[...], across[0:size, :]] + [part[0:size, :] for part in parts])
    pieces[size:, :] = across[size:, :]


def join_kernel(own, part1, part2, part3, chip_slab, mate1, joined):
    del mate1
    size = own.shape[1] // 2
    count = own.shape[0] - size
    for step, part in enumerate((own, part1, part2, part3)):
        joined[piece(step, size), :] = part[0:size, :]
        joined[piece(step, count, 4 * size + 4 * count), :] = part[size:, :]
    joined[4 * size : 4 * size + 4 * count, :] = chip_slab[...]


def split(value):
    high = value.astype(BF16)
    return high, (value - high.astype(F32)).astype(BF16)


def product(left, right):
    return dot(left[0], right[0]) + (dot(left[0], right[1]) + dot(left[1], right[0]))


def row_product(left, right):
    count = left[0].shape[0]
    both = dot(jnp.concatenate(left, axis=0), right[0])
    return both[:count] + (both[count:] + dot(left[0], right[1]))


def symmetric(first, mixed, last):
    return jnp.concatenate(
        [jnp.concatenate([first, mixed], axis=1), jnp.concatenate([mixed.T, last], axis=1)], axis=0
    )


def symmetric_square(high, low):
    half = high.shape[0] // 2
    cross_part = dot(high, low)
    upper = dot(high[:half], high)
    last = dot(high[half:], high[:, half:])
    return symmetric(
        upper[:, :half] + (cross_part[:half, :half] + cross_part[:half, :half].T),
        upper[:, half:] + (cross_part[:half, half:] + cross_part[half:, :half].T),
        last + (cross_part[half:, half:] + cross_part[half:, half:].T),
    )


def symmetric_product(left, right):
    half = left[0].shape[0] // 2
    upper = product((left[0][:half], left[1][:half]), right)
    last = product((left[0][half:], left[1][half:]), (right[0][:, half:], right[1][:, half:]))
    return symmetric(upper[:, :half], upper[:, half:], last)


def finish_kernel(
    total_rows, active, joined_mine, joined_mate, own, mate, across1, mate1, across2, mate2,
    out, gram, highs, lows, factor, left, result, state_flags, sems, out_sems,
):
    chip, core = chip_index(), core_index()
    half, width = across1.shape
    cols = gram.shape[0]
    near, far = pl.multiple_of(chip * half, half), pl.multiple_of((1 - chip) * half, half)
    fetch = pltpu.make_async_copy(active, state_flags, sems.at[6])
    fetch.start()
    every = pl.ds(0, 2 * half)
    copies = [
        pltpu.make_async_copy(source, left.at[where, index * width : (index + 1) * width], sems.at[number])
        for number, (source, where, index) in enumerate(
            [
                (own, every, 0),
                (mate, every, 1),
                (across1, pl.ds(near, half), 2),
                (mate1, pl.ds(near, half), 3),
                (across2, pl.ds(far, half), 2),
                (mate2, pl.ds(far, half), 3),
            ]
        )
    ]
    for copy in copies:
        copy.start()

    def parts(start, stop):
        mine, theirs = joined_mine[start:stop, :], joined_mate[start:stop, :]
        return jnp.where(core == 0, mine, theirs), jnp.where(core == 0, theirs, mine)

    def put(row, col, value):
        gram[row * width : (row + 1) * width, col * width : (col + 1) * width] = value

    count = 3 * width // 2
    chip_first = 2 * width
    other_first = chip_first + count
    middle = other_first + count // 2
    here = parts(chip_first, other_first)
    upper, lower = parts(other_first, middle), parts(middle, other_first + count)
    there = [jnp.concatenate([upper[index], lower[1 - index]], axis=0) for index in range(2)]
    for side in range(2):
        core0, core1 = [jnp.where(chip == side, near_part, far_part) for near_part, far_part in zip(here, there)]
        between = jnp.concatenate([core0[width:], core1[width:]], axis=0)
        put(2 * side, 2 * side, core0[:width])
        put(2 * side + 1, 2 * side + 1, core1[:width])
        put(2 * side, 2 * side + 1, between)
        put(2 * side + 1, 2 * side, between.T)
    core0, core1 = parts(0, 2 * width)
    top0, low0, top1, low1 = core0[:width], core0[width:], core1[:width], core1[width:]
    off10 = jnp.where(chip == 0, low0, low1)
    off01 = jnp.where(chip == 0, low1, low0)
    put(0, 2, top0)
    put(1, 3, top1)
    put(0, 3, off01)
    put(1, 2, off10)
    put(2, 0, top0.T)
    put(3, 1, top1.T)
    put(3, 0, off01.T)
    put(2, 1, off10.T)

    fetch.wait()
    states = active.shape[0]
    vecs = cols // states
    col_state = lax.broadcasted_iota(jnp.int32, (1, cols), 1) // vecs
    flags = jnp.zeros((1, cols), F32)
    for state in range(states):
        flags = jnp.where(col_state == state, state_flags[state].astype(F32), flags)
    square = jnp.zeros((vecs, cols), F32)
    for state in range(states):
        rows = slice(state * vecs, (state + 1) * vecs)
        kept = jnp.where(jnp.logical_and(flags != 0, state_flags[state] != 0), gram[rows, :], 0.0)
        diagonal = lax.broadcasted_iota(jnp.int32, (vecs, cols), 0) + state * vecs == lax.broadcasted_iota(
            jnp.int32, (vecs, cols), 1
        )
        kept = kept + jnp.where(diagonal, (1.0 - flags) * total_rows, 0.0)
        gram[rows, :] = kept
        square = square + kept * kept
    frob_square = jnp.sum(jnp.sum(square, axis=0, keepdims=True), axis=1, keepdims=True)
    frob_norm = jnp.sqrt(frob_square)
    inverse_norm = 1.0 / frob_norm

    current = gram[...] * inverse_norm
    start = (2 * chip + core) * width
    last = ITERS - 2
    for step in range(last):
        high, low = split(current)
        highs[step], lows[step] = high, low
        square = symmetric_square(high, low)
        cube = symmetric_product((high, low), split(square))
        current = 2.25 * current - 1.5 * square + 0.25 * cube
    highs[last], lows[last] = split(current)
    gram[...] = current

    def times(step, slab):
        return row_product(split(slab), (highs[step], lows[step]))

    def newton(step, slab):
        return 1.5 * slab - 0.5 * times(step, slab)

    row_id = lax.broadcasted_iota(jnp.int32, (width, cols), 0) + start
    col_id = lax.broadcasted_iota(jnp.int32, (width, cols), 1)
    unit = jnp.where(row_id == col_id, 1.0, 0.0)
    slab = 1.5 * unit - 0.5 * gram[pl.ds(pl.multiple_of(start, width), width), :]
    slab = 1.5 * unit - 0.5 * times(last, newton(last, slab))
    for step in range(last, -1, -1):
        slab = newton(step, slab)
    slab = slab * jnp.sqrt(total_rows / frob_norm)

    factor[...] = jnp.where(flags != 0, slab, unit).T.astype(BF16)

    def block(index):
        return factor[pl.ds(pl.multiple_of(index * width, width), width), :]

    weights = jnp.concatenate(
        [
            block(2 * chip + core),
            block(2 * chip + 1 - core),
            block(2 * (1 - chip) + core),
            block(2 * (1 - chip) + 1 - core),
        ],
        axis=0,
    )
    for copy in copies:
        copy.wait()
    pieces = out_sems.shape[0]
    size = out.shape[0] // pieces
    stores = []
    for piece in range(pieces):
        rows = slice(piece * size, (piece + 1) * size)
        result[rows, :] = dot(left[rows, :], weights).astype(BF16)
        stores.append(pltpu.make_async_copy(result.at[rows, :], out.at[rows, :], out_sems.at[piece]))
        stores[-1].start()
    for store in stores:
        store.wait()


def shards(vectors, active):
    rows, width = vectors.shape
    half = rows // 2
    row_devices = lax.axis_size("row")
    total_rows = rows * row_devices
    cols = width * lax.axis_size("state")
    chip = chip_index()
    size = width // 2
    shape = jax.ShapeDtypeStruct

    def swap(value, bit):
        return lax.ppermute(value, "state", [(index, index ^ bit) for index in range(4)])

    def move(value, bits, chips=0):
        pairs = []
        for state_from in range(4):
            for row_from in range(row_devices):
                state_to = state_from ^ ((2 if row_from % 4 < 2 else 3) if chips else 0)
                pairs.append((state_from * row_devices + row_from, state_to * row_devices + (row_from ^ bits)))
        return lax.ppermute(value, ("state", "row"), pairs)

    def after(value, other):
        return call(
            pass_kernel, shape(value.shape, value.dtype), 0, 0, "after", in_specs=[ANY, ANY], out_specs=ANY,
            aliases={0: 0},
        )(value, other)

    across1 = swap(lax.dynamic_slice_in_dim(vectors, (1 - chip) * half, half, 0), 2)
    mate = swap(vectors, 1)
    quarter = 3 * width // 8
    small = shape((quarter, width), F32)
    keep, *sends = call(
        chip_gram_kernel, (small,) * 4, 2, 0, "chip_gram", scratch=[pltpu.VMEM((4 * quarter, width), F32)]
    )(vectors, mate)
    later = call(
        later_kernel, shape((half, width), BF16), 0, 0, "later", scratch=[pltpu.SemaphoreType.DMA],
        in_specs=[ANY, ANY], out_specs=ANY,
    )(vectors, keep)
    across2 = swap(later, 2)

    groups = [4 * index for index in range(row_devices // 4)]
    parts = [move(sends[step - 1], step) for step in (3, 2, 1)][::-1]
    chip_sum = call(chip_sum_kernel, small, 4, 0, "chip_sum", in_specs=[VMEM] * 4 + [ANY])(keep, *parts, later)
    chip_parts = [chip_sum] + [move(chip_sum, bits) for bits in groups[1:]]
    pair, both = shape((size, width), F32), shape((size + quarter, width), F32)
    chip_piece, keep, *sends = call(
        pair_gram_kernel, (small, pair, both, both, both), 3 + len(chip_parts), 0, "pair_gram",
        scratch=[pltpu.VMEM((4 * size, width), F32)],
    )(vectors, mate, across1, *chip_parts)
    parts = [move(sends[step - 1], step) for step in (3, 2, 1)][::-1]
    pair_sum, payload, chip_slab = call(
        group_sum_kernel, (pair, both, shape((4 * quarter, width), F32)), 5, 0, "group_sum"
    )(keep, chip_piece, *parts)
    mate1 = swap(after(across1, pair_sum), 1)
    pair_parts = [move(payload, bits, chips) for bits in groups for chips in range(2) if bits or chips]
    pieces = call(pair_sum_kernel, both, 1 + len(pair_parts), 0, "pair_sum")(pair_sum, *pair_parts)
    parts = [move(pieces, step) for step in (1, 2, 3)]
    mate2 = swap(after(across2, pieces), 1)
    joined_mine = call(
        join_kernel, shape((4 * (size + 2 * quarter), width), F32), 0, 0, "join", in_specs=[VMEM] * 5 + [ANY]
    )(pieces, *parts, chip_slab, mate1)
    joined_mate = swap(joined_mine, 1)

    return call(
        functools.partial(finish_kernel, float(total_rows)),
        shape((rows, width), BF16),
        0,
        12 * cols**3 * 3 + 2 * rows * cols * width,
        "finish",
        scratch=[
            pltpu.VMEM((cols, cols), F32),
            pltpu.VMEM((ITERS - 1, cols, cols), BF16),
            pltpu.VMEM((ITERS - 1, cols, cols), BF16),
            pltpu.VMEM((cols, width), BF16),
            pltpu.VMEM((rows, cols), BF16),
            pltpu.VMEM((rows, width), BF16),
            pltpu.SMEM(active.shape, jnp.int32),
            pltpu.SemaphoreType.DMA((7,)),
            pltpu.SemaphoreType.DMA((4,)),
        ],
        in_specs=[ANY, VMEM, VMEM] + [ANY] * 6,
        out_specs=ANY,
        mib=24,
    )(
        active, joined_mine, joined_mate, vectors, mate, across1, mate1, across2, mate2
    )


def solution(mesh):
    in_specs = (P("row", "state"), P())
    out_specs = P("row", "state")
    return jax.shard_map(shards, mesh=mesh, in_specs=in_specs, out_specs=out_specs, check_vma=False)
```

```python
import functools

import jax
import jax.numpy as jnp
from jax import lax
from jax.experimental import pallas as pl
from jax.experimental.pallas import tpu as pltpu
from jax.sharding import PartitionSpec as P

ITERS = 5
F32 = jnp.float32
BF16 = jnp.bfloat16
VMEM = pl.BlockSpec(memory_space=pltpu.VMEM)
ANY = pl.BlockSpec(memory_space=pl.ANY)


def dot(left, right):
    return jnp.dot(left, right, preferred_element_type=F32)


def cross(left, right):
    return lax.dot_general(left, right, (((0,), (0,)), ((), ())), preferred_element_type=F32)


def call(kernel, out_shape, n_args, flops, name, scratch=(), in_specs=None, out_specs=None, mib=12, aliases=None):
    return pl.pallas_call(
        kernel,
        out_shape=out_shape,
        in_specs=in_specs or [VMEM] * n_args,
        out_specs=out_specs or jax.tree.map(lambda _: VMEM, out_shape),
        scratch_shapes=list(scratch),
        input_output_aliases=aliases or {},
        compiler_params=pltpu.CompilerParams(vmem_limit_bytes=mib * 2**20),
        cost_estimate=pl.CostEstimate(flops=0, bytes_accessed=0, transcendentals=0),
        name=name,
    )


def chip_index():
    return lax.axis_index("state") // 2


def core_index():
    return lax.axis_index("state") % 2


def piece(step, size, base=0):
    member = lax.bitwise_xor(lax.axis_index("row") % 4, jnp.int32(step))
    return pl.ds(pl.multiple_of(base + member * size, size), size)


def tree_sum(values):
    while len(values) > 1:
        values = [left + right for left, right in zip(values[::2], values[1::2])]
    return values[0]


def later_kernel(own, after, part, sem):
    del after
    size = part.shape[0]
    copy = pltpu.make_async_copy(own.at[pl.ds(pl.multiple_of(chip_index() * size, size), size), :], part, sem)
    copy.start()
    copy.wait()


def chip_gram_kernel(own, mate, keep, send1, send2, send3, slab):
    core = core_index()
    width = own.shape[1]
    size = keep.shape[0]
    between = cross(own[...], mate[...])
    slab[0:width, :] = cross(own[...], own[...])
    slab[width:, :] = jnp.where(core == 0, between[: width // 2, :], between.T[width // 2 :, :])
    for step, out in enumerate((keep, send1, send2, send3)):
        out[...] = slab[piece(step, size), :]


def chip_sum_kernel(keep, part1, part2, part3, later, total):
    del later
    total[...] = tree_sum([keep[...], part1[...], part2[...], part3[...]])


def pair_gram_kernel(own, mate, across, *rest):
    chip_parts, (chip_piece, keep, send1, send2, send3, slab) = rest[:-6], rest[-6:]
    chip = chip_index()
    half, width = across.shape
    size = keep.shape[0]
    rows = pl.ds(pl.multiple_of(chip * half, half), half)
    same = cross(across[...], own[rows, :])
    other = cross(across[...], mate[rows, :])
    slab[0:width, :] = jnp.where(chip == 0, same.T, same)
    slab[width : 2 * width, :] = jnp.where(chip == 0, other.T, other)
    chip_sum = tree_sum([part[...] for part in chip_parts])
    chip_piece[...] = chip_sum
    keep[...] = slab[piece(0, size), :]
    for step, out in enumerate((send1, send2, send3)):
        out[0:size, :] = slab[piece(step + 1, size), :]
        out[size:, :] = chip_sum


def pass_kernel(value, after, same):
    del value, after, same


def group_sum_kernel(keep, chip_piece, part1, part2, part3, total, payload, chip_slab):
    size, count = keep.shape[0], chip_piece.shape[0]
    parts = (part1, part2, part3)
    group_sum = tree_sum([keep[...]] + [part[0:size, :] for part in parts])
    total[...] = group_sum
    payload[0:size, :] = group_sum
    payload[size:, :] = chip_piece[...]
    chip_slab[piece(0, count), :] = chip_piece[...]
    for step, part in enumerate(parts):
        chip_slab[piece(step + 1, count), :] = part[size:, :]


def pair_sum_kernel(total, across, *rest):
    parts, pieces = rest[:-1], rest[-1]
    size = total.shape[0]
    pieces[0:size, :] = tree_sum([total[...], across[0:size, :]] + [part[0:size, :] for part in parts])
    pieces[size:, :] = across[size:, :]


def join_kernel(own, part1, part2, part3, chip_slab, joined):
    size = own.shape[1] // 2
    count = own.shape[0] - size
    for step, part in enumerate((own, part1, part2, part3)):
        joined[piece(step, size), :] = part[0:size, :]
        joined[piece(step, count, 4 * size + 4 * count), :] = part[size:, :]
    joined[4 * size : 4 * size + 4 * count, :] = chip_slab[...]


def split(value):
    high = value.astype(BF16)
    return high, (value - high.astype(F32)).astype(BF16)


def product(left, right):
    return dot(
        jnp.concatenate([left[0], left[0], left[1]], axis=1), jnp.concatenate([right[0], right[1], right[0]], axis=0)
    )


def row_product(left, right):
    count = left[0].shape[0]
    both = dot(jnp.concatenate(left, axis=0), right[0])
    return both[:count] + (both[count:] + dot(left[0], right[1]))


def symmetric(first, mixed, last):
    return jnp.concatenate(
        [jnp.concatenate([first, mixed], axis=1), jnp.concatenate([mixed.T, last], axis=1)], axis=0
    )


def symmetric_square(high, low):
    half = high.shape[0] // 2
    cross_part = dot(high, low)
    upper = dot(high[:half], high)
    last = dot(high[half:], high[:, half:])
    return symmetric(
        upper[:, :half] + (cross_part[:half, :half] + cross_part[:half, :half].T),
        upper[:, half:] + (cross_part[:half, half:] + cross_part[half:, :half].T),
        last + (cross_part[half:, half:] + cross_part[half:, half:].T),
    )


def symmetric_product(left, right):
    half = left[0].shape[0] // 2
    upper = product((left[0][:half], left[1][:half]), right)
    last = product((left[0][half:], left[1][half:]), (right[0][:, half:], right[1][:, half:]))
    return symmetric(upper[:, :half], upper[:, half:], last)


def finish_kernel(
    total_rows, active, joined_mine, joined_mate, own, mate, across1, mate1, across2, mate2,
    out, gram, highs, lows, factor, result, state_flags, fetch_sem, out_sems,
):
    chip, core = chip_index(), core_index()
    half, width = across1.shape
    cols = gram.shape[0]
    fetch = pltpu.make_async_copy(active, state_flags, fetch_sem)
    fetch.start()

    def parts(start, stop):
        mine, theirs = joined_mine[start:stop, :], joined_mate[start:stop, :]
        return jnp.where(core == 0, mine, theirs), jnp.where(core == 0, theirs, mine)

    def put(row, col, value):
        gram[row * width : (row + 1) * width, col * width : (col + 1) * width] = value

    count = 3 * width // 2
    chip_first = 2 * width
    other_first = chip_first + count
    middle = other_first + count // 2
    here = parts(chip_first, other_first)
    upper, lower = parts(other_first, middle), parts(middle, other_first + count)
    there = [jnp.concatenate([upper[index], lower[1 - index]], axis=0) for index in range(2)]
    for side in range(2):
        core0, core1 = [jnp.where(chip == side, near_part, far_part) for near_part, far_part in zip(here, there)]
        between = jnp.concatenate([core0[width:], core1[width:]], axis=0)
        put(2 * side, 2 * side, core0[:width])
        put(2 * side + 1, 2 * side + 1, core1[:width])
        put(2 * side, 2 * side + 1, between)
        put(2 * side + 1, 2 * side, between.T)
    core0, core1 = parts(0, 2 * width)
    top0, low0, top1, low1 = core0[:width], core0[width:], core1[:width], core1[width:]
    off10 = jnp.where(chip == 0, low0, low1)
    off01 = jnp.where(chip == 0, low1, low0)
    put(0, 2, top0)
    put(1, 3, top1)
    put(0, 3, off01)
    put(1, 2, off10)
    put(2, 0, top0.T)
    put(3, 1, top1.T)
    put(3, 0, off01.T)
    put(2, 1, off10.T)

    fetch.wait()
    states = active.shape[0]
    vecs = cols // states
    col_state = lax.broadcasted_iota(jnp.int32, (1, cols), 1) // vecs
    flags = jnp.zeros((1, cols), F32)
    for state in range(states):
        flags = jnp.where(col_state == state, state_flags[state].astype(F32), flags)
    square = jnp.zeros((vecs, cols), F32)
    for state in range(states):
        rows = slice(state * vecs, (state + 1) * vecs)
        kept = jnp.where(jnp.logical_and(flags != 0, state_flags[state] != 0), gram[rows, :], 0.0)
        diagonal = lax.broadcasted_iota(jnp.int32, (vecs, cols), 0) + state * vecs == lax.broadcasted_iota(
            jnp.int32, (vecs, cols), 1
        )
        kept = kept + jnp.where(diagonal, (1.0 - flags) * total_rows, 0.0)
        gram[rows, :] = kept
        square = square + kept * kept
    frob_square = jnp.sum(jnp.sum(square, axis=0, keepdims=True), axis=1, keepdims=True)
    frob_norm = jnp.sqrt(frob_square)
    inverse_norm = 1.0 / frob_norm

    current = gram[...] * inverse_norm
    start = (2 * chip + core) * width
    last = ITERS - 2
    for step in range(last):
        high, low = split(current)
        highs[step], lows[step] = high, low
        square = symmetric_square(high, low)
        cube = symmetric_product((high, low), split(square))
        current = 2.25 * current - 1.5 * square + 0.25 * cube
    highs[last], lows[last] = split(current)
    gram[...] = current

    def times(step, slab):
        return row_product(split(slab), (highs[step], lows[step]))

    def newton(step, slab):
        return 1.5 * slab - 0.5 * times(step, slab)

    row_id = lax.broadcasted_iota(jnp.int32, (width, cols), 0) + start
    col_id = lax.broadcasted_iota(jnp.int32, (width, cols), 1)
    unit = jnp.where(row_id == col_id, 1.0, 0.0)
    slab = 1.5 * unit - 0.5 * gram[pl.ds(pl.multiple_of(start, width), width), :]
    slab = 1.5 * unit - 0.5 * times(last, newton(last, slab))
    for step in range(last, -1, -1):
        slab = newton(step, slab)
    slab = slab * jnp.sqrt(total_rows / frob_norm)

    factor[...] = jnp.where(flags != 0, slab, unit).T.astype(BF16)

    def block(index):
        return factor[pl.ds(pl.multiple_of(index * width, width), width), :]

    weights = jnp.concatenate(
        [
            block(2 * chip + core),
            block(2 * chip + 1 - core),
            block(2 * (1 - chip) + core),
            block(2 * (1 - chip) + 1 - core),
        ],
        axis=0,
    )
    pieces = out_sems.shape[0] // 2
    size = half // pieces
    stores = []
    for part, (across, other) in enumerate(((across1, mate1), (across2, mate2))):
        start = half * (chip if part == 0 else 1 - chip)
        for index in range(pieces):
            near = slice(index * size, (index + 1) * size)
            rows = pl.ds(pl.multiple_of(start + index * size, size), size)
            left = jnp.concatenate([own[rows, :], mate[rows, :], across[near, :], other[near, :]], axis=1)
            result[rows, :] = dot(left, weights).astype(BF16)
            stores.append(
                pltpu.make_async_copy(result.at[rows, :], out.at[rows, :], out_sems.at[part * pieces + index])
            )
            stores[-1].start()
    for store in stores:
        store.wait()


def shards(vectors, active):
    rows, width = vectors.shape
    half = rows // 2
    row_devices = lax.axis_size("row")
    total_rows = rows * row_devices
    cols = width * lax.axis_size("state")
    chip = chip_index()
    size = width // 2
    shape = jax.ShapeDtypeStruct

    def swap(value, bit):
        return lax.ppermute(value, "state", [(index, index ^ bit) for index in range(4)])

    def move(value, bits, chips=0):
        pairs = []
        for state_from in range(4):
            for row_from in range(row_devices):
                state_to = state_from ^ ((2 if row_from % 4 < 2 else 3) if chips else 0)
                pairs.append((state_from * row_devices + row_from, state_to * row_devices + (row_from ^ bits)))
        return lax.ppermute(value, ("state", "row"), pairs)

    def after(value, other):
        return call(
            pass_kernel, shape(value.shape, value.dtype), 0, 0, "after", in_specs=[ANY, ANY], out_specs=ANY,
            aliases={0: 0},
        )(value, other)

    across1 = swap(lax.dynamic_slice_in_dim(vectors, (1 - chip) * half, half, 0), 2)
    mate = swap(vectors, 1)
    quarter = 3 * width // 8
    small = shape((quarter, width), F32)
    keep, *sends = call(
        chip_gram_kernel, (small,) * 4, 2, 0, "chip_gram", scratch=[pltpu.VMEM((4 * quarter, width), F32)]
    )(vectors, mate)
    later = call(
        later_kernel, shape((half, width), BF16), 0, 0, "later", scratch=[pltpu.SemaphoreType.DMA],
        in_specs=[ANY, ANY], out_specs=ANY,
    )(vectors, keep)
    across2 = swap(later, 2)

    groups = [4 * index for index in range(row_devices // 4)]
    parts = [move(sends[step - 1], step) for step in (3, 2, 1)][::-1]
    chip_sum = call(chip_sum_kernel, small, 4, 0, "chip_sum", in_specs=[VMEM] * 4 + [ANY])(keep, *parts, later)
    chip_parts = [chip_sum] + [move(chip_sum, bits) for bits in groups[1:]]
    pair, both = shape((size, width), F32), shape((size + quarter, width), F32)
    chip_piece, keep, *sends = call(
        pair_gram_kernel, (small, pair, both, both, both), 3 + len(chip_parts), 0, "pair_gram",
        scratch=[pltpu.VMEM((4 * size, width), F32)],
    )(vectors, mate, across1, *chip_parts)
    parts = [move(sends[step - 1], step) for step in (3, 2, 1)][::-1]
    pair_sum, payload, chip_slab = call(
        group_sum_kernel, (pair, both, shape((4 * quarter, width), F32)), 5, 0, "group_sum"
    )(keep, chip_piece, *parts)
    pair_parts = [move(payload, bits, chips) for bits in groups for chips in range(2) if bits or chips]
    pieces = call(pair_sum_kernel, both, 1 + len(pair_parts), 0, "pair_sum")(pair_sum, *pair_parts)
    parts = [move(pieces, step) for step in (1, 2, 3)]
    mate2 = swap(after(across2, pieces), 1)
    mate1 = swap(after(across1, pieces), 1)
    joined_mine = call(join_kernel, shape((4 * (size + 2 * quarter), width), F32), 5, 0, "join")(
        pieces, *parts, chip_slab
    )
    joined_mate = swap(joined_mine, 1)

    return call(
        functools.partial(finish_kernel, float(total_rows)),
        shape((rows, width), BF16),
        0,
        12 * cols**3 * 3 + 2 * rows * cols * width,
        "finish",
        scratch=[
            pltpu.VMEM((cols, cols), F32),
            pltpu.VMEM((ITERS - 1, cols, cols), BF16),
            pltpu.VMEM((ITERS - 1, cols, cols), BF16),
            pltpu.VMEM((cols, width), BF16),
            pltpu.VMEM((rows, width), BF16),
            pltpu.SMEM(active.shape, jnp.int32),
            pltpu.SemaphoreType.DMA,
            pltpu.SemaphoreType.DMA((4,)),
        ],
        in_specs=[ANY] + [VMEM] * 8,
        out_specs=ANY,
        mib=24,
    )(
        active, joined_mine, joined_mate, vectors, mate, across1, mate1, across2, mate2
    )


def solution(mesh):
    in_specs = (P("row", "state"), P())
    out_specs = P("row", "state")
    return jax.shard_map(shards, mesh=mesh, in_specs=in_specs, out_specs=out_specs, check_vma=False)
```

```python
import functools

import jax
import jax.numpy as jnp
from jax import lax
from jax.experimental import pallas as pl
from jax.experimental.pallas import tpu as pltpu
from jax.sharding import PartitionSpec as P

ITERS = 5
F32 = jnp.float32
BF16 = jnp.bfloat16
VMEM = pl.BlockSpec(memory_space=pltpu.VMEM)
ANY = pl.BlockSpec(memory_space=pl.ANY)


def dot(left, right):
    return jnp.dot(left, right, preferred_element_type=F32)


def cross(left, right):
    return lax.dot_general(left, right, (((0,), (0,)), ((), ())), preferred_element_type=F32)


def call(kernel, out_shape, n_args, flops, name, scratch=(), in_specs=None, out_specs=None, mib=12, aliases=None):
    return pl.pallas_call(
        kernel,
        out_shape=out_shape,
        in_specs=in_specs or [VMEM] * n_args,
        out_specs=out_specs or jax.tree.map(lambda _: VMEM, out_shape),
        scratch_shapes=list(scratch),
        input_output_aliases=aliases or {},
        compiler_params=pltpu.CompilerParams(vmem_limit_bytes=mib * 2**20),
        cost_estimate=pl.CostEstimate(flops=0, bytes_accessed=0, transcendentals=0),
        name=name,
    )


def chip_index():
    return lax.axis_index("state") // 2


def core_index():
    return lax.axis_index("state") % 2


def piece(step, size, base=0):
    member = lax.bitwise_xor(lax.axis_index("row") % 4, jnp.int32(step))
    return pl.ds(pl.multiple_of(base + member * size, size), size)


def tree_sum(values):
    while len(values) > 1:
        values = [left + right for left, right in zip(values[::2], values[1::2])]
    return values[0]


def later_kernel(own, after, part, sem):
    del after
    size = part.shape[0]
    copy = pltpu.make_async_copy(own.at[pl.ds(pl.multiple_of(chip_index() * size, size), size), :], part, sem)
    copy.start()
    copy.wait()


def chip_gram_kernel(own, mate, keep, send1, send2, send3, slab):
    core = core_index()
    width = own.shape[1]
    size = keep.shape[0]
    between = cross(own[...], mate[...])
    slab[0:width, :] = cross(own[...], own[...])
    slab[width:, :] = jnp.where(core == 0, between[: width // 2, :], between.T[width // 2 :, :])
    for step, out in enumerate((keep, send1, send2, send3)):
        out[...] = slab[piece(step, size), :]


def chip_sum_kernel(keep, part1, part2, part3, later, total):
    del later
    total[...] = tree_sum([keep[...], part1[...], part2[...], part3[...]])


def pair_gram_kernel(own, mate, across, *rest):
    chip_parts, (chip_piece, keep, send1, send2, send3, slab) = rest[:-6], rest[-6:]
    chip = chip_index()
    half, width = across.shape
    size = keep.shape[0]
    rows = pl.ds(pl.multiple_of(chip * half, half), half)
    same = cross(across[...], own[rows, :])
    other = cross(across[...], mate[rows, :])
    slab[0:width, :] = jnp.where(chip == 0, same.T, same)
    slab[width : 2 * width, :] = jnp.where(chip == 0, other.T, other)
    chip_sum = tree_sum([part[...] for part in chip_parts])
    chip_piece[...] = chip_sum
    keep[...] = slab[piece(0, size), :]
    for step, out in enumerate((send1, send2, send3)):
        out[0:size, :] = slab[piece(step + 1, size), :]
        out[size:, :] = chip_sum


def pass_kernel(value, after, same):
    del value, after, same


def group_sum_kernel(keep, chip_piece, part1, part2, part3, total, payload, chip_slab):
    size, count = keep.shape[0], chip_piece.shape[0]
    parts = (part1, part2, part3)
    group_sum = tree_sum([keep[...]] + [part[0:size, :] for part in parts])
    total[...] = group_sum
    payload[0:size, :] = group_sum
    payload[size:, :] = chip_piece[...]
    chip_slab[piece(0, count), :] = chip_piece[...]
    for step, part in enumerate(parts):
        chip_slab[piece(step + 1, count), :] = part[size:, :]


def pair_sum_kernel(total, across, *rest):
    parts, pieces = rest[:-1], rest[-1]
    size = total.shape[0]
    pieces[0:size, :] = tree_sum([total[...], across[0:size, :]] + [part[0:size, :] for part in parts])
    pieces[size:, :] = across[size:, :]


def join_kernel(own, part1, part2, part3, chip_slab, joined):
    size = own.shape[1] // 2
    count = own.shape[0] - size
    for step, part in enumerate((own, part1, part2, part3)):
        joined[piece(step, size), :] = part[0:size, :]
        joined[piece(step, count, 4 * size + 4 * count), :] = part[size:, :]
    joined[4 * size : 4 * size + 4 * count, :] = chip_slab[...]


def split(value):
    high = value.astype(BF16)
    return high, (value - high.astype(F32)).astype(BF16)


def product(left, right):
    return dot(
        jnp.concatenate([left[0], left[0], left[1]], axis=1), jnp.concatenate([right[0], right[1], right[0]], axis=0)
    )


def row_product(left, right):
    count = left[0].shape[0]
    both = dot(jnp.concatenate(left, axis=0), right[0])
    return both[:count] + (both[count:] + dot(left[0], right[1]))


def symmetric(first, mixed, last):
    return jnp.concatenate(
        [jnp.concatenate([first, mixed], axis=1), jnp.concatenate([mixed.T, last], axis=1)], axis=0
    )


def symmetric_product(left, right):
    half = left[0].shape[0] // 2
    upper = product((left[0][:half], left[1][:half]), right)
    last = product((left[0][half:], left[1][half:]), (right[0][:, half:], right[1][:, half:]))
    return symmetric(upper[:, :half], upper[:, half:], last)


def finish_kernel(
    total_rows, active, joined_mine, joined_mate, own, mate, across1, mate1, across2, mate2,
    out, gram, highs, lows, factor, result, state_flags, fetch_sem, out_sems,
):
    chip, core = chip_index(), core_index()
    half, width = across1.shape
    cols = gram.shape[0]
    fetch = pltpu.make_async_copy(active, state_flags, fetch_sem)
    fetch.start()

    def parts(start, stop):
        mine, theirs = joined_mine[start:stop, :], joined_mate[start:stop, :]
        return jnp.where(core == 0, mine, theirs), jnp.where(core == 0, theirs, mine)

    def put(row, col, value):
        gram[row * width : (row + 1) * width, col * width : (col + 1) * width] = value

    count = 3 * width // 2
    chip_first = 2 * width
    other_first = chip_first + count
    middle = other_first + count // 2
    here = parts(chip_first, other_first)
    upper, lower = parts(other_first, middle), parts(middle, other_first + count)
    there = [jnp.concatenate([upper[index], lower[1 - index]], axis=0) for index in range(2)]
    for side in range(2):
        core0, core1 = [jnp.where(chip == side, near_part, far_part) for near_part, far_part in zip(here, there)]
        between = jnp.concatenate([core0[width:], core1[width:]], axis=0)
        put(2 * side, 2 * side, core0[:width])
        put(2 * side + 1, 2 * side + 1, core1[:width])
        put(2 * side, 2 * side + 1, between)
        put(2 * side + 1, 2 * side, between.T)
    core0, core1 = parts(0, 2 * width)
    top0, low0, top1, low1 = core0[:width], core0[width:], core1[:width], core1[width:]
    off10 = jnp.where(chip == 0, low0, low1)
    off01 = jnp.where(chip == 0, low1, low0)
    put(0, 2, top0)
    put(1, 3, top1)
    put(0, 3, off01)
    put(1, 2, off10)
    put(2, 0, top0.T)
    put(3, 1, top1.T)
    put(3, 0, off01.T)
    put(2, 1, off10.T)

    fetch.wait()
    states = active.shape[0]
    vecs = cols // states
    col_state = lax.broadcasted_iota(jnp.int32, (1, cols), 1) // vecs
    flags = jnp.zeros((1, cols), F32)
    for state in range(states):
        flags = jnp.where(col_state == state, state_flags[state].astype(F32), flags)
    square = jnp.zeros((vecs, cols), F32)
    for state in range(states):
        rows = slice(state * vecs, (state + 1) * vecs)
        kept = jnp.where(jnp.logical_and(flags != 0, state_flags[state] != 0), gram[rows, :], 0.0)
        diagonal = lax.broadcasted_iota(jnp.int32, (vecs, cols), 0) + state * vecs == lax.broadcasted_iota(
            jnp.int32, (vecs, cols), 1
        )
        kept = kept + jnp.where(diagonal, (1.0 - flags) * total_rows, 0.0)
        gram[rows, :] = kept
        square = square + kept * kept
    frob_square = jnp.sum(jnp.sum(square, axis=0, keepdims=True), axis=1, keepdims=True)
    frob_norm = jnp.sqrt(frob_square)
    inverse_norm = 1.0 / frob_norm

    current = gram[...] * inverse_norm
    start = (2 * chip + core) * width
    last = ITERS - 2
    for step in range(last):
        high, low = split(current)
        highs[step], lows[step] = high, low
        square = symmetric_product((high, low), (high, low))
        cube = symmetric_product((high, low), split(square))
        current = 2.25 * current - 1.5 * square + 0.25 * cube
    highs[last], lows[last] = split(current)
    gram[...] = current

    def times(step, slab):
        return row_product(split(slab), (highs[step], lows[step]))

    def newton(step, slab):
        return 1.5 * slab - 0.5 * times(step, slab)

    row_id = lax.broadcasted_iota(jnp.int32, (width, cols), 0) + start
    col_id = lax.broadcasted_iota(jnp.int32, (width, cols), 1)
    unit = jnp.where(row_id == col_id, 1.0, 0.0)
    slab = 1.5 * unit - 0.5 * gram[pl.ds(pl.multiple_of(start, width), width), :]
    slab = 1.5 * unit - 0.5 * times(last, newton(last, slab))
    for step in range(last, -1, -1):
        slab = newton(step, slab)
    slab = slab * jnp.sqrt(total_rows / frob_norm)

    factor[...] = jnp.where(flags != 0, slab, unit).T.astype(BF16)

    def block(index):
        return factor[pl.ds(pl.multiple_of(index * width, width), width), :]

    weights = jnp.concatenate(
        [
            block(2 * chip + core),
            block(2 * chip + 1 - core),
            block(2 * (1 - chip) + core),
            block(2 * (1 - chip) + 1 - core),
        ],
        axis=0,
    )
    pieces = out_sems.shape[0] // 2
    size = half // pieces
    stores = []
    for part, (across, other) in enumerate(((across1, mate1), (across2, mate2))):
        start = half * (chip if part == 0 else 1 - chip)
        for index in range(pieces):
            near = slice(index * size, (index + 1) * size)
            rows = pl.ds(pl.multiple_of(start + index * size, size), size)
            left = jnp.concatenate([own[rows, :], mate[rows, :], across[near, :], other[near, :]], axis=1)
            result[rows, :] = dot(left, weights).astype(BF16)
            stores.append(
                pltpu.make_async_copy(result.at[rows, :], out.at[rows, :], out_sems.at[part * pieces + index])
            )
            stores[-1].start()
    for store in stores:
        store.wait()


def shards(vectors, active):
    rows, width = vectors.shape
    half = rows // 2
    row_devices = lax.axis_size("row")
    total_rows = rows * row_devices
    cols = width * lax.axis_size("state")
    chip = chip_index()
    size = width // 2
    shape = jax.ShapeDtypeStruct

    def swap(value, bit):
        return lax.ppermute(value, "state", [(index, index ^ bit) for index in range(4)])

    def move(value, bits, chips=0):
        pairs = []
        for state_from in range(4):
            for row_from in range(row_devices):
                state_to = state_from ^ ((2 if row_from % 4 < 2 else 3) if chips else 0)
                pairs.append((state_from * row_devices + row_from, state_to * row_devices + (row_from ^ bits)))
        return lax.ppermute(value, ("state", "row"), pairs)

    def after(value, other):
        return call(
            pass_kernel, shape(value.shape, value.dtype), 0, 0, "after", in_specs=[ANY, ANY], out_specs=ANY,
            aliases={0: 0},
        )(value, other)

    across1 = swap(lax.dynamic_slice_in_dim(vectors, (1 - chip) * half, half, 0), 2)
    mate = swap(vectors, 1)
    quarter = 3 * width // 8
    small = shape((quarter, width), F32)
    keep, *sends = call(
        chip_gram_kernel, (small,) * 4, 2, 0, "chip_gram", scratch=[pltpu.VMEM((4 * quarter, width), F32)]
    )(vectors, mate)
    later = call(
        later_kernel, shape((half, width), BF16), 0, 0, "later", scratch=[pltpu.SemaphoreType.DMA],
        in_specs=[ANY, ANY], out_specs=ANY,
    )(vectors, keep)
    across2 = swap(later, 2)

    groups = [4 * index for index in range(row_devices // 4)]
    parts = [move(sends[step - 1], step) for step in (3, 2, 1)][::-1]
    chip_sum = call(chip_sum_kernel, small, 4, 0, "chip_sum", in_specs=[VMEM] * 4 + [ANY])(keep, *parts, later)
    chip_parts = [chip_sum] + [move(chip_sum, bits) for bits in groups[1:]]
    pair, both = shape((size, width), F32), shape((size + quarter, width), F32)
    chip_piece, keep, *sends = call(
        pair_gram_kernel, (small, pair, both, both, both), 3 + len(chip_parts), 0, "pair_gram",
        scratch=[pltpu.VMEM((4 * size, width), F32)],
    )(vectors, mate, across1, *chip_parts)
    parts = [move(sends[step - 1], step) for step in (3, 2, 1)][::-1]
    pair_sum, payload, chip_slab = call(
        group_sum_kernel, (pair, both, shape((4 * quarter, width), F32)), 5, 0, "group_sum"
    )(keep, chip_piece, *parts)
    pair_parts = [move(payload, bits, chips) for bits in groups for chips in range(2) if bits or chips]
    pieces = call(pair_sum_kernel, both, 1 + len(pair_parts), 0, "pair_sum")(pair_sum, *pair_parts)
    parts = [move(pieces, step) for step in (1, 2, 3)]
    mate2 = swap(after(across2, pieces), 1)
    mate1 = swap(after(across1, pieces), 1)
    joined_mine = call(join_kernel, shape((4 * (size + 2 * quarter), width), F32), 5, 0, "join")(
        pieces, *parts, chip_slab
    )
    joined_mate = swap(joined_mine, 1)

    return call(
        functools.partial(finish_kernel, float(total_rows)),
        shape((rows, width), BF16),
        0,
        12 * cols**3 * 3 + 2 * rows * cols * width,
        "finish",
        scratch=[
            pltpu.VMEM((cols, cols), F32),
            pltpu.VMEM((ITERS - 1, cols, cols), BF16),
            pltpu.VMEM((ITERS - 1, cols, cols), BF16),
            pltpu.VMEM((cols, width), BF16),
            pltpu.VMEM((rows, width), BF16),
            pltpu.SMEM(active.shape, jnp.int32),
            pltpu.SemaphoreType.DMA,
            pltpu.SemaphoreType.DMA((4,)),
        ],
        in_specs=[ANY] + [VMEM] * 8,
        out_specs=ANY,
        mib=24,
    )(
        active, joined_mine, joined_mate, vectors, mate, across1, mate1, across2, mate2
    )


def solution(mesh):
    in_specs = (P("row", "state"), P())
    out_specs = P("row", "state")
    return jax.shard_map(shards, mesh=mesh, in_specs=in_specs, out_specs=out_specs, check_vma=False)
```

```python
import functools

import jax
import jax.numpy as jnp
from jax import lax
from jax.experimental import pallas as pl
from jax.experimental.pallas import tpu as pltpu
from jax.sharding import PartitionSpec as P

ITERS = 5
PAIR_COST = 14 * 10**9
JOIN_COST = 15 * 10**8
F32 = jnp.float32
BF16 = jnp.bfloat16
VMEM = pl.BlockSpec(memory_space=pltpu.VMEM)
ANY = pl.BlockSpec(memory_space=pl.ANY)


def dot(left, right):
    return jnp.dot(left, right, preferred_element_type=F32)


def cross(left, right):
    return lax.dot_general(left, right, (((0,), (0,)), ((), ())), preferred_element_type=F32)


def call(kernel, out_shape, n_args, flops, name, scratch=(), in_specs=None, out_specs=None, mib=12, aliases=None):
    return pl.pallas_call(
        kernel,
        out_shape=out_shape,
        in_specs=in_specs or [VMEM] * n_args,
        out_specs=out_specs or jax.tree.map(lambda _: VMEM, out_shape),
        scratch_shapes=list(scratch),
        input_output_aliases=aliases or {},
        compiler_params=pltpu.CompilerParams(vmem_limit_bytes=mib * 2**20),
        cost_estimate=pl.CostEstimate(flops=flops, bytes_accessed=0, transcendentals=0),
        name=name,
    )


def chip_index():
    return lax.axis_index("state") // 2


def core_index():
    return lax.axis_index("state") % 2


def piece(step, size, base=0):
    member = lax.bitwise_xor(lax.axis_index("row") % 4, jnp.int32(step))
    return pl.ds(pl.multiple_of(base + member * size, size), size)


def tree_sum(values):
    while len(values) > 1:
        values = [left + right for left, right in zip(values[::2], values[1::2])]
    return values[0]


def later_kernel(own, after, part, sem):
    del after
    size = part.shape[0]
    copy = pltpu.make_async_copy(own.at[pl.ds(pl.multiple_of(chip_index() * size, size), size), :], part, sem)
    copy.start()
    copy.wait()


def chip_gram_kernel(own, mate, keep, send1, send2, send3, slab):
    core = core_index()
    width = own.shape[1]
    size = keep.shape[0]
    between = cross(own[...], mate[...])
    slab[0:width, :] = cross(own[...], own[...])
    slab[width:, :] = jnp.where(core == 0, between[: width // 2, :], between.T[width // 2 :, :])
    for step, out in enumerate((keep, send1, send2, send3)):
        out[...] = slab[piece(step, size), :]


def chip_sum_kernel(keep, part1, part2, part3, later, total):
    del later
    total[...] = tree_sum([keep[...], part1[...], part2[...], part3[...]])


def pair_gram_kernel(own, mate, across, *rest):
    chip_parts, (chip_piece, keep, send1, send2, send3, slab) = rest[:-6], rest[-6:]
    chip = chip_index()
    half, width = across.shape
    size = keep.shape[0]
    rows = pl.ds(pl.multiple_of(chip * half, half), half)
    same = cross(across[...], own[rows, :])
    other = cross(across[...], mate[rows, :])
    slab[0:width, :] = jnp.where(chip == 0, same.T, same)
    slab[width : 2 * width, :] = jnp.where(chip == 0, other.T, other)
    chip_sum = tree_sum([part[...] for part in chip_parts])
    chip_piece[...] = chip_sum
    keep[...] = slab[piece(0, size), :]
    for step, out in enumerate((send1, send2, send3)):
        out[0:size, :] = slab[piece(step + 1, size), :]
        out[size:, :] = chip_sum


def pass_kernel(value, after, same):
    del value, after, same


def group_sum_kernel(keep, chip_piece, part1, part2, part3, total, payload, chip_slab):
    size, count = keep.shape[0], chip_piece.shape[0]
    parts = (part1, part2, part3)
    group_sum = tree_sum([keep[...]] + [part[0:size, :] for part in parts])
    total[...] = group_sum
    payload[0:size, :] = group_sum
    payload[size:, :] = chip_piece[...]
    chip_slab[piece(0, count), :] = chip_piece[...]
    for step, part in enumerate(parts):
        chip_slab[piece(step + 1, count), :] = part[size:, :]


def pair_sum_kernel(total, across, *rest):
    parts, pieces = rest[:-1], rest[-1]
    size = total.shape[0]
    pieces[0:size, :] = tree_sum([total[...], across[0:size, :]] + [part[0:size, :] for part in parts])
    pieces[size:, :] = across[size:, :]


def join_kernel(own, part1, part2, part3, chip_slab, joined):
    size = own.shape[1] // 2
    count = own.shape[0] - size
    for step, part in enumerate((own, part1, part2, part3)):
        joined[piece(step, size), :] = part[0:size, :]
        joined[piece(step, count, 4 * size + 4 * count), :] = part[size:, :]
    joined[4 * size : 4 * size + 4 * count, :] = chip_slab[...]


def split(value):
    high = value.astype(BF16)
    return high, (value - high.astype(F32)).astype(BF16)


def product(left, right):
    return dot(
        jnp.concatenate([left[0], left[0], left[1]], axis=1), jnp.concatenate([right[0], right[1], right[0]], axis=0)
    )


def row_product(left, right):
    count = left[0].shape[0]
    both = dot(jnp.concatenate(left, axis=0), right[0])
    return both[:count] + (both[count:] + dot(left[0], right[1]))


def symmetric(first, mixed, last):
    return jnp.concatenate(
        [jnp.concatenate([first, mixed], axis=1), jnp.concatenate([mixed.T, last], axis=1)], axis=0
    )


def symmetric_product(left, right):
    half = left[0].shape[0] // 2
    upper = product((left[0][:half], left[1][:half]), right)
    last = product((left[0][half:], left[1][half:]), (right[0][:, half:], right[1][:, half:]))
    return symmetric(upper[:, :half], upper[:, half:], last)


def finish_kernel(
    total_rows, active, joined_mine, joined_mate, own, mate, across1, mate1, across2, mate2,
    out, gram, highs, lows, factor, result, state_flags, fetch_sem, out_sems,
):
    chip, core = chip_index(), core_index()
    half, width = across1.shape
    cols = gram.shape[0]
    fetch = pltpu.make_async_copy(active, state_flags, fetch_sem)
    fetch.start()

    def parts(start, stop):
        mine, theirs = joined_mine[start:stop, :], joined_mate[start:stop, :]
        return jnp.where(core == 0, mine, theirs), jnp.where(core == 0, theirs, mine)

    def put(row, col, value):
        gram[row * width : (row + 1) * width, col * width : (col + 1) * width] = value

    count = 3 * width // 2
    chip_first = 2 * width
    other_first = chip_first + count
    middle = other_first + count // 2
    here = parts(chip_first, other_first)
    upper, lower = parts(other_first, middle), parts(middle, other_first + count)
    there = [jnp.concatenate([upper[index], lower[1 - index]], axis=0) for index in range(2)]
    for side in range(2):
        core0, core1 = [jnp.where(chip == side, near_part, far_part) for near_part, far_part in zip(here, there)]
        between = jnp.concatenate([core0[width:], core1[width:]], axis=0)
        put(2 * side, 2 * side, core0[:width])
        put(2 * side + 1, 2 * side + 1, core1[:width])
        put(2 * side, 2 * side + 1, between)
        put(2 * side + 1, 2 * side, between.T)
    core0, core1 = parts(0, 2 * width)
    top0, low0, top1, low1 = core0[:width], core0[width:], core1[:width], core1[width:]
    off10 = jnp.where(chip == 0, low0, low1)
    off01 = jnp.where(chip == 0, low1, low0)
    put(0, 2, top0)
    put(1, 3, top1)
    put(0, 3, off01)
    put(1, 2, off10)
    put(2, 0, top0.T)
    put(3, 1, top1.T)
    put(3, 0, off01.T)
    put(2, 1, off10.T)

    fetch.wait()
    states = active.shape[0]
    vecs = cols // states
    col_state = lax.broadcasted_iota(jnp.int32, (1, cols), 1) // vecs
    flags = jnp.zeros((1, cols), F32)
    for state in range(states):
        flags = jnp.where(col_state == state, state_flags[state].astype(F32), flags)
    square = jnp.zeros((vecs, cols), F32)
    for state in range(states):
        rows = slice(state * vecs, (state + 1) * vecs)
        kept = jnp.where(jnp.logical_and(flags != 0, state_flags[state] != 0), gram[rows, :], 0.0)
        diagonal = lax.broadcasted_iota(jnp.int32, (vecs, cols), 0) + state * vecs == lax.broadcasted_iota(
            jnp.int32, (vecs, cols), 1
        )
        kept = kept + jnp.where(diagonal, (1.0 - flags) * total_rows, 0.0)
        gram[rows, :] = kept
        square = square + kept * kept
    frob_square = jnp.sum(jnp.sum(square, axis=0, keepdims=True), axis=1, keepdims=True)
    frob_norm = jnp.sqrt(frob_square)
    inverse_norm = 1.0 / frob_norm

    current = gram[...] * inverse_norm
    start = (2 * chip + core) * width
    last = ITERS - 2
    for step in range(last):
        high, low = split(current)
        highs[step], lows[step] = high, low
        square = symmetric_product((high, low), (high, low))
        cube = symmetric_product((high, low), split(square))
        current = 2.25 * current - 1.5 * square + 0.25 * cube
    highs[last], lows[last] = split(current)
    gram[...] = current

    def times(step, slab):
        return row_product(split(slab), (highs[step], lows[step]))

    def newton(step, slab):
        return 1.5 * slab - 0.5 * times(step, slab)

    row_id = lax.broadcasted_iota(jnp.int32, (width, cols), 0) + start
    col_id = lax.broadcasted_iota(jnp.int32, (width, cols), 1)
    unit = jnp.where(row_id == col_id, 1.0, 0.0)
    slab = 1.5 * unit - 0.5 * gram[pl.ds(pl.multiple_of(start, width), width), :]
    slab = 1.5 * unit - 0.5 * times(last, newton(last, slab))
    for step in range(last, -1, -1):
        slab = newton(step, slab)
    slab = slab * jnp.sqrt(total_rows / frob_norm)

    factor[...] = jnp.where(flags != 0, slab, unit).T.astype(BF16)

    def block(index):
        return factor[pl.ds(pl.multiple_of(index * width, width), width), :]

    weights = jnp.concatenate(
        [
            block(2 * chip + core),
            block(2 * chip + 1 - core),
            block(2 * (1 - chip) + core),
            block(2 * (1 - chip) + 1 - core),
        ],
        axis=0,
    )
    pieces = out_sems.shape[0] // 2
    size = half // pieces
    stores = []
    for part, (across, other) in enumerate(((across1, mate1), (across2, mate2))):
        start = half * (chip if part == 0 else 1 - chip)
        for index in range(pieces):
            near = slice(index * size, (index + 1) * size)
            rows = pl.ds(pl.multiple_of(start + index * size, size), size)
            left = jnp.concatenate([own[rows, :], mate[rows, :], across[near, :], other[near, :]], axis=1)
            result[rows, :] = dot(left, weights).astype(BF16)
            stores.append(
                pltpu.make_async_copy(result.at[rows, :], out.at[rows, :], out_sems.at[part * pieces + index])
            )
            stores[-1].start()
    for store in stores:
        store.wait()


def shards(vectors, active):
    rows, width = vectors.shape
    half = rows // 2
    row_devices = lax.axis_size("row")
    total_rows = rows * row_devices
    cols = width * lax.axis_size("state")
    chip = chip_index()
    size = width // 2
    shape = jax.ShapeDtypeStruct

    def swap(value, bit):
        return lax.ppermute(value, "state", [(index, index ^ bit) for index in range(4)])

    def move(value, bits, chips=0):
        pairs = []
        for state_from in range(4):
            for row_from in range(row_devices):
                state_to = state_from ^ ((2 if row_from % 4 < 2 else 3) if chips else 0)
                pairs.append((state_from * row_devices + row_from, state_to * row_devices + (row_from ^ bits)))
        return lax.ppermute(value, ("state", "row"), pairs)

    def after(value, other):
        return call(
            pass_kernel, shape(value.shape, value.dtype), 0, 0, "after", in_specs=[ANY, ANY], out_specs=ANY,
            aliases={0: 0},
        )(value, other)

    across1 = swap(lax.dynamic_slice_in_dim(vectors, (1 - chip) * half, half, 0), 2)
    mate = swap(vectors, 1)
    quarter = 3 * width // 8
    small = shape((quarter, width), F32)
    keep, *sends = call(
        chip_gram_kernel, (small,) * 4, 2, 0, "chip_gram", scratch=[pltpu.VMEM((4 * quarter, width), F32)]
    )(vectors, mate)
    later = call(
        later_kernel, shape((half, width), BF16), 0, 0, "later", scratch=[pltpu.SemaphoreType.DMA],
        in_specs=[ANY, ANY], out_specs=ANY,
    )(vectors, keep)
    across2 = swap(later, 2)

    groups = [4 * index for index in range(row_devices // 4)]
    parts = [move(sends[step - 1], step) for step in (3, 2, 1)][::-1]
    chip_sum = call(chip_sum_kernel, small, 4, 0, "chip_sum", in_specs=[VMEM] * 4 + [ANY])(keep, *parts, later)
    chip_parts = [chip_sum] + [move(chip_sum, bits) for bits in groups[1:]]
    pair, both = shape((size, width), F32), shape((size + quarter, width), F32)
    chip_piece, keep, *sends = call(
        pair_gram_kernel, (small, pair, both, both, both), 3 + len(chip_parts), PAIR_COST, "pair_gram",
        scratch=[pltpu.VMEM((4 * size, width), F32)],
    )(vectors, mate, across1, *chip_parts)
    parts = [move(sends[step - 1], step) for step in (3, 2, 1)][::-1]
    pair_sum, payload, chip_slab = call(
        group_sum_kernel, (pair, both, shape((4 * quarter, width), F32)), 5, 0, "group_sum"
    )(keep, chip_piece, *parts)
    pair_parts = [move(payload, bits, chips) for bits in groups for chips in range(2) if bits or chips]
    pieces = call(pair_sum_kernel, both, 1 + len(pair_parts), 0, "pair_sum")(pair_sum, *pair_parts)
    parts = [move(pieces, step) for step in (1, 2, 3)]
    mate2 = swap(after(across2, pieces), 1)
    mate1 = swap(after(across1, pieces), 1)
    joined_mine = call(join_kernel, shape((4 * (size + 2 * quarter), width), F32), 5, JOIN_COST, "join")(
        pieces, *parts, chip_slab
    )
    joined_mate = swap(joined_mine, 1)

    return call(
        functools.partial(finish_kernel, float(total_rows)),
        shape((rows, width), BF16),
        0,
        0,
        "finish",
        scratch=[
            pltpu.VMEM((cols, cols), F32),
            pltpu.VMEM((ITERS - 1, cols, cols), BF16),
            pltpu.VMEM((ITERS - 1, cols, cols), BF16),
            pltpu.VMEM((cols, width), BF16),
            pltpu.VMEM((rows, width), BF16),
            pltpu.SMEM(active.shape, jnp.int32),
            pltpu.SemaphoreType.DMA,
            pltpu.SemaphoreType.DMA((4,)),
        ],
        in_specs=[ANY] + [VMEM] * 8,
        out_specs=ANY,
        mib=24,
    )(
        active, joined_mine, joined_mate, vectors, mate, across1, mate1, across2, mate2
    )


def solution(mesh):
    in_specs = (P("row", "state"), P())
    out_specs = P("row", "state")
    return jax.shard_map(shards, mesh=mesh, in_specs=in_specs, out_specs=out_specs, check_vma=False)
```

```python
import functools

import jax
import jax.numpy as jnp
from jax import lax
from jax.experimental import pallas as pl
from jax.experimental.pallas import tpu as pltpu
from jax.sharding import PartitionSpec as P

ITERS = 5
PAIR_COST = 14 * 10**9
JOIN_COST = 15 * 10**8
F32 = jnp.float32
BF16 = jnp.bfloat16
VMEM = pl.BlockSpec(memory_space=pltpu.VMEM)
ANY = pl.BlockSpec(memory_space=pl.ANY)


def dot(left, right):
    return jnp.dot(left, right, preferred_element_type=F32)


def cross(left, right):
    return lax.dot_general(left, right, (((0,), (0,)), ((), ())), preferred_element_type=F32)


def call(kernel, out_shape, n_args, flops, name, scratch=(), in_specs=None, out_specs=None, mib=12, aliases=None):
    return pl.pallas_call(
        kernel,
        out_shape=out_shape,
        in_specs=in_specs or [VMEM] * n_args,
        out_specs=out_specs or jax.tree.map(lambda _: VMEM, out_shape),
        scratch_shapes=list(scratch),
        input_output_aliases=aliases or {},
        compiler_params=pltpu.CompilerParams(vmem_limit_bytes=mib * 2**20),
        cost_estimate=pl.CostEstimate(flops=flops, bytes_accessed=0, transcendentals=0),
        name=name,
    )


def chip_index():
    return lax.axis_index("state") // 2


def core_index():
    return lax.axis_index("state") % 2


def piece(step, size, base=0):
    member = lax.bitwise_xor(lax.axis_index("row") % 4, jnp.int32(step))
    return pl.ds(pl.multiple_of(base + member * size, size), size)


def tree_sum(values):
    while len(values) > 1:
        values = [left + right for left, right in zip(values[::2], values[1::2])]
    return values[0]


def later_kernel(own, after, part, sem):
    del after
    size = part.shape[0]
    copy = pltpu.make_async_copy(own.at[pl.ds(pl.multiple_of(chip_index() * size, size), size), :], part, sem)
    copy.start()
    copy.wait()


def chip_gram_kernel(own, mate, keep, send1, send2, send3, slab):
    core = core_index()
    width = own.shape[1]
    size = keep.shape[0]
    both = cross(own[...], jnp.concatenate([own[...], mate[...]], axis=1))
    between = both[:, width:]
    slab[0:width, :] = both[:, :width]
    slab[width:, :] = jnp.where(core == 0, between[: width // 2, :], between.T[width // 2 :, :])
    for step, out in enumerate((keep, send1, send2, send3)):
        out[...] = slab[piece(step, size), :]


def chip_sum_kernel(keep, part1, part2, part3, later, total):
    del later
    total[...] = tree_sum([keep[...], part1[...], part2[...], part3[...]])


def pair_gram_kernel(own, mate, across, *rest):
    chip_parts, (chip_piece, keep, send1, send2, send3, slab) = rest[:-6], rest[-6:]
    chip = chip_index()
    half, width = across.shape
    size = keep.shape[0]
    rows = pl.ds(pl.multiple_of(chip * half, half), half)
    both = cross(across[...], jnp.concatenate([own[rows, :], mate[rows, :]], axis=1))
    same, other = both[:, :width], both[:, width:]
    slab[0:width, :] = jnp.where(chip == 0, same.T, same)
    slab[width : 2 * width, :] = jnp.where(chip == 0, other.T, other)
    chip_sum = tree_sum([part[...] for part in chip_parts])
    chip_piece[...] = chip_sum
    keep[...] = slab[piece(0, size), :]
    for step, out in enumerate((send1, send2, send3)):
        out[0:size, :] = slab[piece(step + 1, size), :]
        out[size:, :] = chip_sum


def pass_kernel(value, after, same):
    del value, after, same


def group_sum_kernel(keep, chip_piece, part1, part2, part3, total, payload, chip_slab):
    size, count = keep.shape[0], chip_piece.shape[0]
    parts = (part1, part2, part3)
    group_sum = tree_sum([keep[...]] + [part[0:size, :] for part in parts])
    total[...] = group_sum
    payload[0:size, :] = group_sum
    payload[size:, :] = chip_piece[...]
    chip_slab[piece(0, count), :] = chip_piece[...]
    for step, part in enumerate(parts):
        chip_slab[piece(step + 1, count), :] = part[size:, :]


def pair_sum_kernel(total, across, *rest):
    parts, pieces = rest[:-1], rest[-1]
    size = total.shape[0]
    pieces[0:size, :] = tree_sum([total[...], across[0:size, :]] + [part[0:size, :] for part in parts])
    pieces[size:, :] = across[size:, :]


def join_kernel(own, part1, part2, part3, chip_slab, joined):
    size = own.shape[1] // 2
    count = own.shape[0] - size
    for step, part in enumerate((own, part1, part2, part3)):
        joined[piece(step, size), :] = part[0:size, :]
        joined[piece(step, count, 4 * size + 4 * count), :] = part[size:, :]
    joined[4 * size : 4 * size + 4 * count, :] = chip_slab[...]


def split(value):
    high = value.astype(BF16)
    return high, (value - high.astype(F32)).astype(BF16)


def product(left, right):
    return dot(
        jnp.concatenate([left[0], left[0], left[1]], axis=1), jnp.concatenate([right[0], right[1], right[0]], axis=0)
    )


def row_product(left, right):
    count = left[0].shape[0]
    both = dot(jnp.concatenate(left, axis=0), right[0])
    return both[:count] + (both[count:] + dot(left[0], right[1]))


def symmetric(first, mixed, last):
    return jnp.concatenate(
        [jnp.concatenate([first, mixed], axis=1), jnp.concatenate([mixed.T, last], axis=1)], axis=0
    )


def symmetric_product(left, right):
    half = left[0].shape[0] // 2
    upper = product((left[0][:half], left[1][:half]), right)
    last = product((left[0][half:], left[1][half:]), (right[0][:, half:], right[1][:, half:]))
    return symmetric(upper[:, :half], upper[:, half:], last)


def finish_kernel(
    total_rows, active, joined_mine, joined_mate, own, mate, across1, mate1, across2, mate2,
    out, gram, highs, lows, factor, result, state_flags, fetch_sem, out_sems,
):
    chip, core = chip_index(), core_index()
    half, width = across1.shape
    cols = gram.shape[0]
    fetch = pltpu.make_async_copy(active, state_flags, fetch_sem)
    fetch.start()

    def parts(start, stop):
        mine, theirs = joined_mine[start:stop, :], joined_mate[start:stop, :]
        return jnp.where(core == 0, mine, theirs), jnp.where(core == 0, theirs, mine)

    def put(row, col, value):
        gram[row * width : (row + 1) * width, col * width : (col + 1) * width] = value

    count = 3 * width // 2
    chip_first = 2 * width
    other_first = chip_first + count
    middle = other_first + count // 2
    here = parts(chip_first, other_first)
    upper, lower = parts(other_first, middle), parts(middle, other_first + count)
    there = [jnp.concatenate([upper[index], lower[1 - index]], axis=0) for index in range(2)]
    for side in range(2):
        core0, core1 = [jnp.where(chip == side, near_part, far_part) for near_part, far_part in zip(here, there)]
        between = jnp.concatenate([core0[width:], core1[width:]], axis=0)
        put(2 * side, 2 * side, core0[:width])
        put(2 * side + 1, 2 * side + 1, core1[:width])
        put(2 * side, 2 * side + 1, between)
        put(2 * side + 1, 2 * side, between.T)
    core0, core1 = parts(0, 2 * width)
    top0, low0, top1, low1 = core0[:width], core0[width:], core1[:width], core1[width:]
    off10 = jnp.where(chip == 0, low0, low1)
    off01 = jnp.where(chip == 0, low1, low0)
    put(0, 2, top0)
    put(1, 3, top1)
    put(0, 3, off01)
    put(1, 2, off10)
    put(2, 0, top0.T)
    put(3, 1, top1.T)
    put(3, 0, off01.T)
    put(2, 1, off10.T)

    fetch.wait()
    states = active.shape[0]
    vecs = cols // states
    col_state = lax.broadcasted_iota(jnp.int32, (1, cols), 1) // vecs
    flags = jnp.zeros((1, cols), F32)
    for state in range(states):
        flags = jnp.where(col_state == state, state_flags[state].astype(F32), flags)
    square = jnp.zeros((vecs, cols), F32)
    for state in range(states):
        rows = slice(state * vecs, (state + 1) * vecs)
        kept = jnp.where(jnp.logical_and(flags != 0, state_flags[state] != 0), gram[rows, :], 0.0)
        diagonal = lax.broadcasted_iota(jnp.int32, (vecs, cols), 0) + state * vecs == lax.broadcasted_iota(
            jnp.int32, (vecs, cols), 1
        )
        kept = kept + jnp.where(diagonal, (1.0 - flags) * total_rows, 0.0)
        gram[rows, :] = kept
        square = square + kept * kept
    frob_square = jnp.sum(jnp.sum(square, axis=0, keepdims=True), axis=1, keepdims=True)
    frob_norm = jnp.sqrt(frob_square)
    inverse_norm = 1.0 / frob_norm

    current = gram[...] * inverse_norm
    start = (2 * chip + core) * width
    last = ITERS - 2
    for step in range(last):
        high, low = split(current)
        highs[step], lows[step] = high, low
        square = symmetric_product((high, low), (high, low))
        cube = symmetric_product((high, low), split(square))
        current = 2.25 * current - 1.5 * square + 0.25 * cube
    highs[last], lows[last] = split(current)
    gram[...] = current

    def times(step, slab):
        return row_product(split(slab), (highs[step], lows[step]))

    def newton(step, slab):
        return 1.5 * slab - 0.5 * times(step, slab)

    row_id = lax.broadcasted_iota(jnp.int32, (width, cols), 0) + start
    col_id = lax.broadcasted_iota(jnp.int32, (width, cols), 1)
    unit = jnp.where(row_id == col_id, 1.0, 0.0)
    slab = 1.5 * unit - 0.5 * gram[pl.ds(pl.multiple_of(start, width), width), :]
    slab = 1.5 * unit - 0.5 * times(last, newton(last, slab))
    for step in range(last, -1, -1):
        slab = newton(step, slab)
    slab = slab * jnp.sqrt(total_rows / frob_norm)

    factor[...] = jnp.where(flags != 0, slab, unit).T.astype(BF16)

    def block(index):
        return factor[pl.ds(pl.multiple_of(index * width, width), width), :]

    weights = jnp.concatenate(
        [
            block(2 * chip + core),
            block(2 * chip + 1 - core),
            block(2 * (1 - chip) + core),
            block(2 * (1 - chip) + 1 - core),
        ],
        axis=0,
    )
    pieces = out_sems.shape[0] // 2
    size = half // pieces
    stores = []
    for part, (across, other) in enumerate(((across1, mate1), (across2, mate2))):
        start = half * (chip if part == 0 else 1 - chip)
        for index in range(pieces):
            near = slice(index * size, (index + 1) * size)
            rows = pl.ds(pl.multiple_of(start + index * size, size), size)
            left = jnp.concatenate([own[rows, :], mate[rows, :], across[near, :], other[near, :]], axis=1)
            result[rows, :] = dot(left, weights).astype(BF16)
            stores.append(
                pltpu.make_async_copy(result.at[rows, :], out.at[rows, :], out_sems.at[part * pieces + index])
            )
            stores[-1].start()
    for store in stores:
        store.wait()


def shards(vectors, active):
    rows, width = vectors.shape
    half = rows // 2
    row_devices = lax.axis_size("row")
    total_rows = rows * row_devices
    cols = width * lax.axis_size("state")
    chip = chip_index()
    size = width // 2
    shape = jax.ShapeDtypeStruct

    def swap(value, bit):
        return lax.ppermute(value, "state", [(index, index ^ bit) for index in range(4)])

    def move(value, bits, chips=0):
        pairs = []
        for state_from in range(4):
            for row_from in range(row_devices):
                state_to = state_from ^ ((2 if row_from % 4 < 2 else 3) if chips else 0)
                pairs.append((state_from * row_devices + row_from, state_to * row_devices + (row_from ^ bits)))
        return lax.ppermute(value, ("state", "row"), pairs)

    def after(value, other):
        return call(
            pass_kernel, shape(value.shape, value.dtype), 0, 0, "after", in_specs=[ANY, ANY], out_specs=ANY,
            aliases={0: 0},
        )(value, other)

    across1 = swap(lax.dynamic_slice_in_dim(vectors, (1 - chip) * half, half, 0), 2)
    mate = swap(vectors, 1)
    quarter = 3 * width // 8
    small = shape((quarter, width), F32)
    keep, *sends = call(
        chip_gram_kernel, (small,) * 4, 2, 0, "chip_gram", scratch=[pltpu.VMEM((4 * quarter, width), F32)]
    )(vectors, mate)
    later = call(
        later_kernel, shape((half, width), BF16), 0, 0, "later", scratch=[pltpu.SemaphoreType.DMA],
        in_specs=[ANY, ANY], out_specs=ANY,
    )(vectors, keep)
    across2 = swap(later, 2)

    groups = [4 * index for index in range(row_devices // 4)]
    parts = [move(sends[step - 1], step) for step in (3, 2, 1)][::-1]
    chip_sum = call(chip_sum_kernel, small, 4, 0, "chip_sum", in_specs=[VMEM] * 4 + [ANY])(keep, *parts, later)
    chip_parts = [chip_sum] + [move(chip_sum, bits) for bits in groups[1:]]
    pair, both = shape((size, width), F32), shape((size + quarter, width), F32)
    chip_piece, keep, *sends = call(
        pair_gram_kernel, (small, pair, both, both, both), 3 + len(chip_parts), PAIR_COST, "pair_gram",
        scratch=[pltpu.VMEM((4 * size, width), F32)],
    )(vectors, mate, across1, *chip_parts)
    parts = [move(sends[step - 1], step) for step in (3, 2, 1)][::-1]
    pair_sum, payload, chip_slab = call(
        group_sum_kernel, (pair, both, shape((4 * quarter, width), F32)), 5, 0, "group_sum"
    )(keep, chip_piece, *parts)
    pair_parts = [move(payload, bits, chips) for bits in groups for chips in range(2) if bits or chips]
    pieces = call(pair_sum_kernel, both, 1 + len(pair_parts), 0, "pair_sum")(pair_sum, *pair_parts)
    parts = [move(pieces, step) for step in (1, 2, 3)]
    mate2 = swap(after(across2, pieces), 1)
    mate1 = swap(after(across1, pieces), 1)
    joined_mine = call(join_kernel, shape((4 * (size + 2 * quarter), width), F32), 5, JOIN_COST, "join")(
        pieces, *parts, chip_slab
    )
    joined_mate = swap(joined_mine, 1)

    return call(
        functools.partial(finish_kernel, float(total_rows)),
        shape((rows, width), BF16),
        0,
        0,
        "finish",
        scratch=[
            pltpu.VMEM((cols, cols), F32),
            pltpu.VMEM((ITERS - 1, cols, cols), BF16),
            pltpu.VMEM((ITERS - 1, cols, cols), BF16),
            pltpu.VMEM((cols, width), BF16),
            pltpu.VMEM((rows, width), BF16),
            pltpu.SMEM(active.shape, jnp.int32),
            pltpu.SemaphoreType.DMA,
            pltpu.SemaphoreType.DMA((4,)),
        ],
        in_specs=[ANY] + [VMEM] * 8,
        out_specs=ANY,
        mib=24,
    )(
        active, joined_mine, joined_mate, vectors, mate, across1, mate1, across2, mate2
    )


def solution(mesh):
    in_specs = (P("row", "state"), P())
    out_specs = P("row", "state")
    return jax.shard_map(shards, mesh=mesh, in_specs=in_specs, out_specs=out_specs, check_vma=False)
```

```python
import functools

import jax
import jax.numpy as jnp
from jax import lax
from jax.experimental import pallas as pl
from jax.experimental.pallas import tpu as pltpu
from jax.sharding import PartitionSpec as P

ITERS = 5
PAIR_COST = 14 * 10**9
JOIN_COST = 15 * 10**8
F32 = jnp.float32
BF16 = jnp.bfloat16
VMEM = pl.BlockSpec(memory_space=pltpu.VMEM)
ANY = pl.BlockSpec(memory_space=pl.ANY)


def dot(left, right):
    return jnp.dot(left, right, preferred_element_type=F32)


def cross(left, right):
    return lax.dot_general(left, right, (((0,), (0,)), ((), ())), preferred_element_type=F32)


def call(kernel, out_shape, n_args, flops, name, scratch=(), in_specs=None, out_specs=None, mib=12, aliases=None):
    return pl.pallas_call(
        kernel,
        out_shape=out_shape,
        in_specs=in_specs or [VMEM] * n_args,
        out_specs=out_specs or jax.tree.map(lambda _: VMEM, out_shape),
        scratch_shapes=list(scratch),
        input_output_aliases=aliases or {},
        compiler_params=pltpu.CompilerParams(vmem_limit_bytes=mib * 2**20),
        cost_estimate=pl.CostEstimate(flops=flops, bytes_accessed=0, transcendentals=0),
        name=name,
    )


def chip_index():
    return lax.axis_index("state") // 2


def core_index():
    return lax.axis_index("state") % 2


def piece(step, size, base=0):
    member = lax.bitwise_xor(lax.axis_index("row") % 4, jnp.int32(step))
    return pl.ds(pl.multiple_of(base + member * size, size), size)


def tree_sum(values):
    while len(values) > 1:
        values = [left + right for left, right in zip(values[::2], values[1::2])]
    return values[0]


def later_kernel(own, after, part, sem):
    del after
    size = part.shape[0]
    copy = pltpu.make_async_copy(own.at[pl.ds(pl.multiple_of(chip_index() * size, size), size), :], part, sem)
    copy.start()
    copy.wait()


def chip_gram_kernel(own, mate, keep, send1, send2, send3, slab):
    core = core_index()
    width = own.shape[1]
    size = keep.shape[0]
    both = cross(own[...], jnp.concatenate([own[...], mate[...]], axis=1))
    between = both[:, width:]
    slab[0:width, :] = both[:, :width]
    slab[width:, :] = jnp.where(core == 0, between[: width // 2, :], between.T[width // 2 :, :])
    for step, out in enumerate((keep, send1, send2, send3)):
        out[...] = slab[piece(step, size), :]


def chip_sum_kernel(keep, part1, part2, part3, later, total):
    del later
    total[...] = tree_sum([keep[...], part1[...], part2[...], part3[...]])


def pair_gram_kernel(own, mate, across, *rest):
    chip_parts, (chip_piece, keep, send1, send2, send3, slab) = rest[:-6], rest[-6:]
    chip = chip_index()
    half, width = across.shape
    size = keep.shape[0]
    rows = pl.ds(pl.multiple_of(chip * half, half), half)
    both = cross(across[...], jnp.concatenate([own[rows, :], mate[rows, :]], axis=1))
    same, other = both[:, :width], both[:, width:]
    slab[0:width, :] = jnp.where(chip == 0, same.T, same)
    slab[width : 2 * width, :] = jnp.where(chip == 0, other.T, other)
    chip_sum = tree_sum([part[...] for part in chip_parts])
    chip_piece[...] = chip_sum
    keep[...] = slab[piece(0, size), :]
    for step, out in enumerate((send1, send2, send3)):
        out[0:size, :] = slab[piece(step + 1, size), :]
        out[size:, :] = chip_sum


def pass_kernel(value, after, same):
    del value, after, same


def group_sum_kernel(keep, chip_piece, part1, part2, part3, total, payload, chip_slab):
    size, count = keep.shape[0], chip_piece.shape[0]
    parts = (part1, part2, part3)
    group_sum = tree_sum([keep[...]] + [part[0:size, :] for part in parts])
    total[...] = group_sum
    payload[0:size, :] = group_sum
    payload[size:, :] = chip_piece[...]
    chip_slab[piece(0, count), :] = chip_piece[...]
    for step, part in enumerate(parts):
        chip_slab[piece(step + 1, count), :] = part[size:, :]


def pair_sum_kernel(total, across, *rest):
    parts, pieces = rest[:-1], rest[-1]
    size = total.shape[0]
    pieces[0:size, :] = tree_sum([total[...], across[0:size, :]] + [part[0:size, :] for part in parts])
    pieces[size:, :] = across[size:, :]


def join_kernel(own, part1, part2, part3, chip_slab, joined):
    size = own.shape[1] // 2
    count = own.shape[0] - size
    for step, part in enumerate((own, part1, part2, part3)):
        joined[piece(step, size), :] = part[0:size, :]
        joined[piece(step, count, 4 * size + 4 * count), :] = part[size:, :]
    joined[4 * size : 4 * size + 4 * count, :] = chip_slab[...]


def split(value):
    high = value.astype(BF16)
    return high, (value - high.astype(F32)).astype(BF16)


def product(left, right):
    return dot(
        jnp.concatenate([left[0], left[0], left[1]], axis=1), jnp.concatenate([right[0], right[1], right[0]], axis=0)
    )


def row_product(left, right):
    count = left[0].shape[0]
    both = dot(jnp.concatenate(left, axis=0), right[0])
    return both[:count] + (both[count:] + dot(left[0], right[1]))


def symmetric(upper, last):
    half = last.shape[0]
    return jnp.concatenate([upper, jnp.concatenate([upper[:, half:].T, last], axis=1)], axis=0)


def symmetric_product(left, right):
    half = left[0].shape[0] // 2
    upper = product((left[0][:half], left[1][:half]), right)
    last = product((left[0][half:], left[1][half:]), (right[0][:, half:], right[1][:, half:]))
    return upper, last


def finish_kernel(
    total_rows, active, joined_mine, joined_mate, own, mate, across1, mate1, across2, mate2,
    out, gram, highs, lows, factor, result, state_flags, fetch_sem, out_sems,
):
    chip, core = chip_index(), core_index()
    half, width = across1.shape
    cols = gram.shape[0]
    fetch = pltpu.make_async_copy(active, state_flags, fetch_sem)
    fetch.start()

    def parts(start, stop):
        mine, theirs = joined_mine[start:stop, :], joined_mate[start:stop, :]
        return jnp.where(core == 0, mine, theirs), jnp.where(core == 0, theirs, mine)

    def put(row, col, value):
        gram[row * width : (row + 1) * width, col * width : (col + 1) * width] = value

    count = 3 * width // 2
    chip_first = 2 * width
    other_first = chip_first + count
    middle = other_first + count // 2
    here = parts(chip_first, other_first)
    upper, lower = parts(other_first, middle), parts(middle, other_first + count)
    there = [jnp.concatenate([upper[index], lower[1 - index]], axis=0) for index in range(2)]
    for side in range(2):
        core0, core1 = [jnp.where(chip == side, near_part, far_part) for near_part, far_part in zip(here, there)]
        between = jnp.concatenate([core0[width:], core1[width:]], axis=0)
        put(2 * side, 2 * side, core0[:width])
        put(2 * side + 1, 2 * side + 1, core1[:width])
        put(2 * side, 2 * side + 1, between)
        put(2 * side + 1, 2 * side, between.T)
    core0, core1 = parts(0, 2 * width)
    top0, low0, top1, low1 = core0[:width], core0[width:], core1[:width], core1[width:]
    off10 = jnp.where(chip == 0, low0, low1)
    off01 = jnp.where(chip == 0, low1, low0)
    put(0, 2, top0)
    put(1, 3, top1)
    put(0, 3, off01)
    put(1, 2, off10)
    put(2, 0, top0.T)
    put(3, 1, top1.T)
    put(3, 0, off01.T)
    put(2, 1, off10.T)

    fetch.wait()
    states = active.shape[0]
    vecs = cols // states
    col_state = lax.broadcasted_iota(jnp.int32, (1, cols), 1) // vecs
    flags = jnp.zeros((1, cols), F32)
    for state in range(states):
        flags = jnp.where(col_state == state, state_flags[state].astype(F32), flags)
    square = jnp.zeros((vecs, cols), F32)
    for state in range(states):
        rows = slice(state * vecs, (state + 1) * vecs)
        kept = jnp.where(jnp.logical_and(flags != 0, state_flags[state] != 0), gram[rows, :], 0.0)
        diagonal = lax.broadcasted_iota(jnp.int32, (vecs, cols), 0) + state * vecs == lax.broadcasted_iota(
            jnp.int32, (vecs, cols), 1
        )
        kept = kept + jnp.where(diagonal, (1.0 - flags) * total_rows, 0.0)
        gram[rows, :] = kept
        square = square + kept * kept
    frob_square = jnp.sum(jnp.sum(square, axis=0, keepdims=True), axis=1, keepdims=True)
    frob_norm = jnp.sqrt(frob_square)
    inverse_norm = 1.0 / frob_norm

    current = gram[...] * inverse_norm
    start = (2 * chip + core) * width
    last = ITERS - 2
    for step in range(last):
        high, low = split(current)
        highs[step], lows[step] = high, low
        square = symmetric_product((high, low), (high, low))
        cube = symmetric_product((high, low), split(symmetric(*square)))
        middle = cols // 2
        before = current[:middle], current[middle:, middle:]
        current = symmetric(*[2.25 * old - 1.5 * two + 0.25 * three for old, two, three in zip(before, square, cube)])
    highs[last], lows[last] = split(current)
    gram[...] = current

    def times(step, slab):
        return row_product(split(slab), (highs[step], lows[step]))

    def newton(step, slab):
        return 1.5 * slab - 0.5 * times(step, slab)

    row_id = lax.broadcasted_iota(jnp.int32, (width, cols), 0) + start
    col_id = lax.broadcasted_iota(jnp.int32, (width, cols), 1)
    unit = jnp.where(row_id == col_id, 1.0, 0.0)
    slab = 1.5 * unit - 0.5 * gram[pl.ds(pl.multiple_of(start, width), width), :]
    slab = 1.5 * unit - 0.5 * times(last, newton(last, slab))
    for step in range(last, -1, -1):
        slab = newton(step, slab)
    slab = slab * jnp.sqrt(total_rows / frob_norm)

    factor[...] = jnp.where(flags != 0, slab, unit).T.astype(BF16)

    def block(index):
        return factor[pl.ds(pl.multiple_of(index * width, width), width), :]

    weights = jnp.concatenate(
        [
            block(2 * chip + core),
            block(2 * chip + 1 - core),
            block(2 * (1 - chip) + core),
            block(2 * (1 - chip) + 1 - core),
        ],
        axis=0,
    )
    pieces = out_sems.shape[0] // 2
    size = half // pieces
    stores = []
    for part, (across, other) in enumerate(((across1, mate1), (across2, mate2))):
        start = half * (chip if part == 0 else 1 - chip)
        for index in range(pieces):
            near = slice(index * size, (index + 1) * size)
            rows = pl.ds(pl.multiple_of(start + index * size, size), size)
            left = jnp.concatenate([own[rows, :], mate[rows, :], across[near, :], other[near, :]], axis=1)
            result[rows, :] = dot(left, weights).astype(BF16)
            stores.append(
                pltpu.make_async_copy(result.at[rows, :], out.at[rows, :], out_sems.at[part * pieces + index])
            )
            stores[-1].start()
    for store in stores:
        store.wait()


def shards(vectors, active):
    rows, width = vectors.shape
    half = rows // 2
    row_devices = lax.axis_size("row")
    total_rows = rows * row_devices
    cols = width * lax.axis_size("state")
    chip = chip_index()
    size = width // 2
    shape = jax.ShapeDtypeStruct

    def swap(value, bit):
        return lax.ppermute(value, "state", [(index, index ^ bit) for index in range(4)])

    def move(value, bits, chips=0):
        pairs = []
        for state_from in range(4):
            for row_from in range(row_devices):
                state_to = state_from ^ ((2 if row_from % 4 < 2 else 3) if chips else 0)
                pairs.append((state_from * row_devices + row_from, state_to * row_devices + (row_from ^ bits)))
        return lax.ppermute(value, ("state", "row"), pairs)

    def after(value, other):
        return call(
            pass_kernel, shape(value.shape, value.dtype), 0, 0, "after", in_specs=[ANY, ANY], out_specs=ANY,
            aliases={0: 0},
        )(value, other)

    across1 = swap(lax.dynamic_slice_in_dim(vectors, (1 - chip) * half, half, 0), 2)
    mate = swap(vectors, 1)
    quarter = 3 * width // 8
    small = shape((quarter, width), F32)
    keep, *sends = call(
        chip_gram_kernel, (small,) * 4, 2, 0, "chip_gram", scratch=[pltpu.VMEM((4 * quarter, width), F32)]
    )(vectors, mate)
    later = call(
        later_kernel, shape((half, width), BF16), 0, 0, "later", scratch=[pltpu.SemaphoreType.DMA],
        in_specs=[ANY, ANY], out_specs=ANY,
    )(vectors, keep)
    across2 = swap(later, 2)

    groups = [4 * index for index in range(row_devices // 4)]
    parts = [move(sends[step - 1], step) for step in (3, 2, 1)][::-1]
    chip_sum = call(chip_sum_kernel, small, 4, 0, "chip_sum", in_specs=[VMEM] * 4 + [ANY])(keep, *parts, later)
    chip_parts = [chip_sum] + [move(chip_sum, bits) for bits in groups[1:]]
    pair, both = shape((size, width), F32), shape((size + quarter, width), F32)
    chip_piece, keep, *sends = call(
        pair_gram_kernel, (small, pair, both, both, both), 3 + len(chip_parts), PAIR_COST, "pair_gram",
        scratch=[pltpu.VMEM((4 * size, width), F32)],
    )(vectors, mate, across1, *chip_parts)
    parts = [move(sends[step - 1], step) for step in (3, 2, 1)][::-1]
    pair_sum, payload, chip_slab = call(
        group_sum_kernel, (pair, both, shape((4 * quarter, width), F32)), 5, 0, "group_sum"
    )(keep, chip_piece, *parts)
    pair_parts = [move(payload, bits, chips) for bits in groups for chips in range(2) if bits or chips]
    pieces = call(pair_sum_kernel, both, 1 + len(pair_parts), 0, "pair_sum")(pair_sum, *pair_parts)
    parts = [move(pieces, step) for step in (1, 2, 3)]
    mate2 = swap(after(across2, pieces), 1)
    mate1 = swap(after(across1, pieces), 1)
    joined_mine = call(join_kernel, shape((4 * (size + 2 * quarter), width), F32), 5, JOIN_COST, "join")(
        pieces, *parts, chip_slab
    )
    joined_mate = swap(joined_mine, 1)

    return call(
        functools.partial(finish_kernel, float(total_rows)),
        shape((rows, width), BF16),
        0,
        0,
        "finish",
        scratch=[
            pltpu.VMEM((cols, cols), F32),
            pltpu.VMEM((ITERS - 1, cols, cols), BF16),
            pltpu.VMEM((ITERS - 1, cols, cols), BF16),
            pltpu.VMEM((cols, width), BF16),
            pltpu.VMEM((rows, width), BF16),
            pltpu.SMEM(active.shape, jnp.int32),
            pltpu.SemaphoreType.DMA,
            pltpu.SemaphoreType.DMA((4,)),
        ],
        in_specs=[ANY] + [VMEM] * 8,
        out_specs=ANY,
        mib=24,
    )(
        active, joined_mine, joined_mate, vectors, mate, across1, mate1, across2, mate2
    )


def solution(mesh):
    in_specs = (P("row", "state"), P())
    out_specs = P("row", "state")
    return jax.shard_map(shards, mesh=mesh, in_specs=in_specs, out_specs=out_specs, check_vma=False)
```

```python
import functools

import jax
import jax.numpy as jnp
from jax import lax
from jax.experimental import pallas as pl
from jax.experimental.pallas import tpu as pltpu
from jax.sharding import PartitionSpec as P

ITERS = 5
PAIR_COST = 14 * 10**9
JOIN_COST = 6 * 10**9
F32 = jnp.float32
BF16 = jnp.bfloat16
VMEM = pl.BlockSpec(memory_space=pltpu.VMEM)
ANY = pl.BlockSpec(memory_space=pl.ANY)


def dot(left, right):
    return jnp.dot(left, right, preferred_element_type=F32)


def cross(left, right):
    return lax.dot_general(left, right, (((0,), (0,)), ((), ())), preferred_element_type=F32)


def call(kernel, out_shape, n_args, flops, name, scratch=(), in_specs=None, out_specs=None, mib=12, aliases=None):
    return pl.pallas_call(
        kernel,
        out_shape=out_shape,
        in_specs=in_specs or [VMEM] * n_args,
        out_specs=out_specs or jax.tree.map(lambda _: VMEM, out_shape),
        scratch_shapes=list(scratch),
        input_output_aliases=aliases or {},
        compiler_params=pltpu.CompilerParams(vmem_limit_bytes=mib * 2**20),
        cost_estimate=pl.CostEstimate(flops=flops, bytes_accessed=0, transcendentals=0),
        name=name,
    )


def chip_index():
    return lax.axis_index("state") // 2


def core_index():
    return lax.axis_index("state") % 2


def piece(step, size, base=0):
    member = lax.bitwise_xor(lax.axis_index("row") % 4, jnp.int32(step))
    return pl.ds(pl.multiple_of(base + member * size, size), size)


def tree_sum(values):
    while len(values) > 1:
        values = [left + right for left, right in zip(values[::2], values[1::2])]
    return values[0]


def later_kernel(own, after, part, sem):
    del after
    size = part.shape[0]
    copy = pltpu.make_async_copy(own.at[pl.ds(pl.multiple_of(chip_index() * size, size), size), :], part, sem)
    copy.start()
    copy.wait()


def chip_gram_kernel(own, mate, keep, send1, send2, send3, slab):
    core = core_index()
    width = own.shape[1]
    size = keep.shape[0]
    both = cross(own[...], jnp.concatenate([own[...], mate[...]], axis=1))
    between = both[:, width:]
    slab[0:width, :] = both[:, :width]
    slab[width:, :] = jnp.where(core == 0, between[: width // 2, :], between.T[width // 2 :, :])
    for step, out in enumerate((keep, send1, send2, send3)):
        out[...] = slab[piece(step, size), :]


def chip_sum_kernel(keep, part1, part2, part3, later, total):
    del later
    total[...] = tree_sum([keep[...], part1[...], part2[...], part3[...]])


def pair_gram_kernel(own, mate, across, *rest):
    chip_parts, (chip_piece, keep, send1, send2, send3, slab) = rest[:-6], rest[-6:]
    chip = chip_index()
    half, width = across.shape
    size = keep.shape[0]
    rows = pl.ds(pl.multiple_of(chip * half, half), half)
    both = cross(across[...], jnp.concatenate([own[rows, :], mate[rows, :]], axis=1))
    same, other = both[:, :width], both[:, width:]
    slab[0:width, :] = jnp.where(chip == 0, same.T, same)
    slab[width : 2 * width, :] = jnp.where(chip == 0, other.T, other)
    chip_sum = tree_sum([part[...] for part in chip_parts])
    chip_piece[...] = chip_sum
    keep[...] = slab[piece(0, size), :]
    for step, out in enumerate((send1, send2, send3)):
        out[0:size, :] = slab[piece(step + 1, size), :]
        out[size:, :] = chip_sum


def pass_kernel(value, after, same):
    del value, after, same


def group_sum_kernel(keep, chip_piece, part1, part2, part3, total, payload, chip_slab):
    size, count = keep.shape[0], chip_piece.shape[0]
    parts = (part1, part2, part3)
    group_sum = tree_sum([keep[...]] + [part[0:size, :] for part in parts])
    total[...] = group_sum
    payload[0:size, :] = group_sum
    payload[size:, :] = chip_piece[...]
    chip_slab[piece(0, count), :] = chip_piece[...]
    for step, part in enumerate(parts):
        chip_slab[piece(step + 1, count), :] = part[size:, :]


def pair_sum_kernel(total, across, *rest):
    parts, pieces = rest[:-1], rest[-1]
    size = total.shape[0]
    pieces[0:size, :] = tree_sum([total[...], across[0:size, :]] + [part[0:size, :] for part in parts])
    pieces[size:, :] = across[size:, :]


def join_kernel(own, part1, part2, part3, chip_slab, joined):
    size = own.shape[1] // 2
    count = own.shape[0] - size
    for step, part in enumerate((own, part1, part2, part3)):
        joined[piece(step, size), :] = part[0:size, :]
        joined[piece(step, count, 4 * size + 4 * count), :] = part[size:, :]
    joined[4 * size : 4 * size + 4 * count, :] = chip_slab[...]


def split(value):
    high = value.astype(BF16)
    return high, (value - high.astype(F32)).astype(BF16)


def product(left, right):
    return dot(
        jnp.concatenate([left[0], left[0], left[1]], axis=1), jnp.concatenate([right[0], right[1], right[0]], axis=0)
    )


def row_product(left, right):
    count = left[0].shape[0]
    both = dot(jnp.concatenate(left, axis=0), right[0])
    return both[:count] + (both[count:] + dot(left[0], right[1]))


def symmetric(upper, last):
    half = last.shape[0]
    return jnp.concatenate([upper, jnp.concatenate([upper[:, half:].T, last], axis=1)], axis=0)


def symmetric_product(left, right):
    half = left[0].shape[0] // 2
    upper = product((left[0][:half], left[1][:half]), right)
    last = product((left[0][half:], left[1][half:]), (right[0][:, half:], right[1][:, half:]))
    return upper, last


def finish_kernel(
    total_rows, active, joined_mine, joined_mate, own, mate, across1, mate1, across2, mate2,
    out, gram, highs, lows, factor, result, state_flags, fetch_sem, out_sems,
):
    chip, core = chip_index(), core_index()
    half, width = across1.shape
    cols = gram.shape[0]
    fetch = pltpu.make_async_copy(active, state_flags, fetch_sem)
    fetch.start()

    def parts(start, stop):
        mine, theirs = joined_mine[start:stop, :], joined_mate[start:stop, :]
        return jnp.where(core == 0, mine, theirs), jnp.where(core == 0, theirs, mine)

    def put(row, col, value):
        gram[row * width : (row + 1) * width, col * width : (col + 1) * width] = value

    count = 3 * width // 2
    chip_first = 2 * width
    other_first = chip_first + count
    middle = other_first + count // 2
    here = parts(chip_first, other_first)
    upper, lower = parts(other_first, middle), parts(middle, other_first + count)
    there = [jnp.concatenate([upper[index], lower[1 - index]], axis=0) for index in range(2)]
    for side in range(2):
        core0, core1 = [jnp.where(chip == side, near_part, far_part) for near_part, far_part in zip(here, there)]
        between = jnp.concatenate([core0[width:], core1[width:]], axis=0)
        put(2 * side, 2 * side, core0[:width])
        put(2 * side + 1, 2 * side + 1, core1[:width])
        put(2 * side, 2 * side + 1, between)
        put(2 * side + 1, 2 * side, between.T)
    core0, core1 = parts(0, 2 * width)
    top0, low0, top1, low1 = core0[:width], core0[width:], core1[:width], core1[width:]
    off10 = jnp.where(chip == 0, low0, low1)
    off01 = jnp.where(chip == 0, low1, low0)
    put(0, 2, top0)
    put(1, 3, top1)
    put(0, 3, off01)
    put(1, 2, off10)
    put(2, 0, top0.T)
    put(3, 1, top1.T)
    put(3, 0, off01.T)
    put(2, 1, off10.T)

    fetch.wait()
    states = active.shape[0]
    vecs = cols // states
    col_state = lax.broadcasted_iota(jnp.int32, (1, cols), 1) // vecs
    flags = jnp.zeros((1, cols), F32)
    for state in range(states):
        flags = jnp.where(col_state == state, state_flags[state].astype(F32), flags)
    square = jnp.zeros((vecs, cols), F32)
    for state in range(states):
        rows = slice(state * vecs, (state + 1) * vecs)
        kept = jnp.where(jnp.logical_and(flags != 0, state_flags[state] != 0), gram[rows, :], 0.0)
        diagonal = lax.broadcasted_iota(jnp.int32, (vecs, cols), 0) + state * vecs == lax.broadcasted_iota(
            jnp.int32, (vecs, cols), 1
        )
        kept = kept + jnp.where(diagonal, (1.0 - flags) * total_rows, 0.0)
        gram[rows, :] = kept
        square = square + kept * kept
    frob_square = jnp.sum(jnp.sum(square, axis=0, keepdims=True), axis=1, keepdims=True)
    frob_norm = jnp.sqrt(frob_square)
    inverse_norm = 1.0 / frob_norm

    current = gram[...] * inverse_norm
    start = (2 * chip + core) * width
    last = ITERS - 2
    for step in range(last):
        high, low = split(current)
        highs[step], lows[step] = high, low
        square = symmetric_product((high, low), (high, low))
        cube = symmetric_product((high, low), split(symmetric(*square)))
        middle = cols // 2
        before = current[:middle], current[middle:, middle:]
        current = symmetric(*[2.25 * old - 1.5 * two + 0.25 * three for old, two, three in zip(before, square, cube)])
    highs[last], lows[last] = split(current)
    gram[...] = current

    def times(step, slab):
        return row_product(split(slab), (highs[step], lows[step]))

    def newton(step, slab):
        return 1.5 * slab - 0.5 * times(step, slab)

    row_id = lax.broadcasted_iota(jnp.int32, (width, cols), 0) + start
    col_id = lax.broadcasted_iota(jnp.int32, (width, cols), 1)
    unit = jnp.where(row_id == col_id, 1.0, 0.0)
    slab = 1.5 * unit - 0.5 * gram[pl.ds(pl.multiple_of(start, width), width), :]
    slab = 1.5 * unit - 0.5 * times(last, newton(last, slab))
    for step in range(last, -1, -1):
        slab = newton(step, slab)
    slab = slab * jnp.sqrt(total_rows / frob_norm)

    factor[...] = jnp.where(flags != 0, slab, unit).T.astype(BF16)

    def block(index):
        return factor[pl.ds(pl.multiple_of(index * width, width), width), :]

    weights = jnp.concatenate(
        [
            block(2 * chip + core),
            block(2 * chip + 1 - core),
            block(2 * (1 - chip) + core),
            block(2 * (1 - chip) + 1 - core),
        ],
        axis=0,
    )
    pieces = out_sems.shape[0] // 2
    size = half // pieces
    stores = []
    for part, (across, other) in enumerate(((across1, mate1), (across2, mate2))):
        start = half * (chip if part == 0 else 1 - chip)
        for index in range(pieces):
            near = slice(index * size, (index + 1) * size)
            rows = pl.ds(pl.multiple_of(start + index * size, size), size)
            left = jnp.concatenate([own[rows, :], mate[rows, :], across[near, :], other[near, :]], axis=1)
            result[rows, :] = dot(left, weights).astype(BF16)
            stores.append(
                pltpu.make_async_copy(result.at[rows, :], out.at[rows, :], out_sems.at[part * pieces + index])
            )
            stores[-1].start()
    for store in stores:
        store.wait()


def shards(vectors, active):
    rows, width = vectors.shape
    half = rows // 2
    row_devices = lax.axis_size("row")
    total_rows = rows * row_devices
    cols = width * lax.axis_size("state")
    chip = chip_index()
    size = width // 2
    shape = jax.ShapeDtypeStruct

    def swap(value, bit):
        return lax.ppermute(value, "state", [(index, index ^ bit) for index in range(4)])

    def move(value, bits, chips=0):
        pairs = []
        for state_from in range(4):
            for row_from in range(row_devices):
                state_to = state_from ^ ((2 if row_from % 4 < 2 else 3) if chips else 0)
                pairs.append((state_from * row_devices + row_from, state_to * row_devices + (row_from ^ bits)))
        return lax.ppermute(value, ("state", "row"), pairs)

    def after(value, other):
        return call(
            pass_kernel, shape(value.shape, value.dtype), 0, 0, "after", in_specs=[ANY, ANY], out_specs=ANY,
            aliases={0: 0},
        )(value, other)

    across1 = swap(lax.dynamic_slice_in_dim(vectors, (1 - chip) * half, half, 0), 2)
    mate = swap(vectors, 1)
    quarter = 3 * width // 8
    small = shape((quarter, width), F32)
    keep, *sends = call(
        chip_gram_kernel, (small,) * 4, 2, 0, "chip_gram", scratch=[pltpu.VMEM((4 * quarter, width), F32)]
    )(vectors, mate)
    later = call(
        later_kernel, shape((half, width), BF16), 0, 0, "later", scratch=[pltpu.SemaphoreType.DMA],
        in_specs=[ANY, ANY], out_specs=ANY,
    )(vectors, keep)
    across2 = swap(later, 2)

    groups = [4 * index for index in range(row_devices // 4)]
    parts = [move(sends[step - 1], step) for step in (3, 2, 1)][::-1]
    chip_sum = call(chip_sum_kernel, small, 4, 0, "chip_sum", in_specs=[VMEM] * 4 + [ANY])(keep, *parts, later)
    chip_parts = [chip_sum] + [move(chip_sum, bits) for bits in groups[1:]]
    pair, both = shape((size, width), F32), shape((size + quarter, width), F32)
    chip_piece, keep, *sends = call(
        pair_gram_kernel, (small, pair, both, both, both), 3 + len(chip_parts), PAIR_COST, "pair_gram",
        scratch=[pltpu.VMEM((4 * size, width), F32)],
    )(vectors, mate, across1, *chip_parts)
    parts = [move(sends[step - 1], step) for step in (3, 2, 1)][::-1]
    pair_sum, payload, chip_slab = call(
        group_sum_kernel, (pair, both, shape((4 * quarter, width), F32)), 5, 0, "group_sum"
    )(keep, chip_piece, *parts)
    pair_parts = [move(payload, bits, chips) for bits in groups for chips in range(2) if bits or chips]
    pieces = call(pair_sum_kernel, both, 1 + len(pair_parts), 0, "pair_sum")(pair_sum, *pair_parts)
    parts = [move(pieces, step) for step in (1, 2, 3)]
    mate2 = swap(after(across2, pieces), 1)
    mate1 = swap(after(across1, pieces), 1)
    joined_mine = call(join_kernel, shape((4 * (size + 2 * quarter), width), F32), 5, JOIN_COST, "join")(
        pieces, *parts, chip_slab
    )
    joined_mate = swap(joined_mine, 1)

    return call(
        functools.partial(finish_kernel, float(total_rows)),
        shape((rows, width), BF16),
        0,
        0,
        "finish",
        scratch=[
            pltpu.VMEM((cols, cols), F32),
            pltpu.VMEM((ITERS - 1, cols, cols), BF16),
            pltpu.VMEM((ITERS - 1, cols, cols), BF16),
            pltpu.VMEM((cols, width), BF16),
            pltpu.VMEM((rows, width), BF16),
            pltpu.SMEM(active.shape, jnp.int32),
            pltpu.SemaphoreType.DMA,
            pltpu.SemaphoreType.DMA((4,)),
        ],
        in_specs=[ANY] + [VMEM] * 8,
        out_specs=ANY,
        mib=24,
    )(
        active, joined_mine, joined_mate, vectors, mate, across1, mate1, across2, mate2
    )


def solution(mesh):
    in_specs = (P("row", "state"), P())
    out_specs = P("row", "state")
    return jax.shard_map(shards, mesh=mesh, in_specs=in_specs, out_specs=out_specs, check_vma=False)
```
